128 devices in a mesh: ka: 32 (over x, z, core), ga: 4 (over y).
Axes of the slice: x: 4, y: 4, z: 4, core: 2. Of those that a mesh axis runs over, the one named last changes fastest.
Arguments:
- delta_rho: float32 [2048, 128], P('ka'), may hold values from -1.8 to 1.8
- bloch_blocks: float32 [2048, 2, 8, 6000], P('ka', None, None, 'ga'), may hold values from -1.5 to 1.5
- coulomb: float32 [6000], P('ga'), may hold values from 0.1 to 1
- energies: float32 [2048, 8], P('ka'), may hold values from -4 to 4
- dipole: float32 [2048, 128], P('ka'), may hold values from -3 to 3
- pair_count: int32 [256], replicated, may hold values from 1 to 8, as said below
- pair_target: int32 [256, 8], replicated, may hold values from 0 to 255, as said below
- kernel: float32 [256, 512], replicated, may hold values from -1 to 1
Outputs:
- delta_out: float32 [2048, 128], P('ka')
The draws below stay inside these ranges and needn't reach their ends.
Inputs may be any that keep to these rules, and one draw needn't show every extreme that they name: `pair_count`: the blocks of one device (aligned runs of 8 blocks) always include one with all 8 entries live. `pair_target`: a k-block index; only the first pair_count[b] entries of row b are live. Among the live entries of the 8 blocks of one device, at most 2 have targets within the 8 blocks of any one device; in every draw some device receives exactly 2 live entries from every device.
All inputs are finite; a program needn't handle non-finite values.
Results may differ from the reference program's by a relative error of at most 0.00023.
Values sent between devices are 32-bit elements; how exact they have to be, the bound alone decides.
A program may use at most 64 MiB of HBM per device.

```python
import math
import jax
import jax.numpy as jnp
from jax import lax

NB = 8
NG = 6000
KB = 8
MAXP = 8
STEPS = 3
KPOINTS = 2048
NBLK = 8
NBLOCKS = 256


def pair_layout(key):
    per_dev = NBLOCKS // NBLK
    entries = NBLK * MAXP
    capacity = max(2, (entries + per_dev - 1) // per_dev)
    groups = entries // capacity
    count_key, group_key, order_key, hub_key, local_key = jax.random.split(key, 5)
    counts = jax.random.randint(count_key, (per_dev, NBLK), 1, MAXP + 1)
    chosen = jax.random.randint(group_key, (per_dev,), 0, groups)
    first_entry = chosen * capacity
    offsets = jnp.arange(NBLK) * MAXP
    needed = jnp.clip(first_entry[:, None] + capacity - offsets[None, :], 0, MAXP)
    correlation = (offsets[None, :] < first_entry[:, None] + capacity) & (offsets[None, :] + MAXP > first_entry[:, None])
    counts = jnp.where(correlation, jnp.maximum(counts, needed), counts)
    counts = jnp.where(jnp.arange(NBLK)[None, :] == (first_entry // MAXP)[:, None], MAXP, counts)
    scores = jax.random.randint(order_key, (per_dev, per_dev), 0, 1 << 20) * per_dev + jnp.arange(per_dev)[None, :]
    ranking = jnp.argsort(scores, axis=1)
    hub_device = jax.random.randint(hub_key, (), 0, per_dev)
    destination = ranking[:, :groups]
    at_chosen = jnp.take_along_axis(destination, chosen[:, None], axis=1)
    column = jnp.arange(groups)[None, :]
    destination = jnp.where(column == chosen[:, None], hub_device, jnp.where(destination == hub_device, at_chosen, destination))
    local_block = jax.random.randint(local_key, (per_dev, NBLK, MAXP), 0, NBLK)
    entry_index = jnp.arange(NBLK)[:, None] * MAXP + jnp.arange(MAXP)[None, :]
    target_dev = destination[:, entry_index // capacity]
    target = target_dev * NBLK + local_block
    return (counts.reshape(NBLOCKS).astype(jnp.int32), target.reshape(NBLOCKS, MAXP).astype(jnp.int32))


def draw_pair_count(key, part):
    return pair_layout(jax.random.fold_in(key, 7))[0]


def draw_pair_target(key, part):
    return pair_layout(jax.random.fold_in(key, 7))[1]


def draw_bloch_blocks(key, part):
    key = jax.random.fold_in(key, 11)
    value_key = jax.random.fold_in(key, 0)
    shape = (KPOINTS, 2, NB, NG)
    values = jnp.clip(0.5 * jax.random.normal(value_key, shape, jnp.float32), -1.5, 1.5)
    return values.astype(jnp.float32)


def block_levels(stream_key, extent, cuts, smallest, high):
    loudness, own = 1.0, jax.random.fold_in(stream_key, 6)
    for position, blocks in cuts:
        heights = jnp.exp(jax.random.uniform(jax.random.fold_in(own, position), (blocks,), jnp.float32, smallest / len(cuts), high / len(cuts)))
        loudness = loudness * jnp.repeat(heights, extent[position] // blocks).reshape([-1 if axis == position else 1 for axis in range(len(extent))])
    return loudness


def noise(own_key, extent, spread, most, cuts=(), held_as=jnp.bfloat16):
    factor_of = block_levels(own_key, extent, cuts, -0.22, 0.18) if cuts else 1.0
    values = jax.random.normal(own_key, extent, jnp.float32) * spread * factor_of
    return jnp.minimum(jnp.maximum(values, -most), most).astype(held_as)


def setup_inputs(seed: int = 0) -> dict:
    seeds = jax.random.split(jax.random.key(seed), 9)
    return {
        "delta_rho": noise(seeds[0], (KPOINTS, 2 * NB * NB), 0.3, 1.8, ((0, 32),), jnp.float32),
        "bloch_blocks": draw_bloch_blocks(jax.random.fold_in(seeds[8], 71), 0),
        "coulomb": jnp.clip(jnp.exp(math.log(1.0) - 2.3025851 * jax.random.uniform(seeds[2], (NG,), jnp.float32) ** block_levels(seeds[2], (NG,), ((0, 4),), -0.2, 0.2)), 0.1, 1.0),
        "energies": jnp.clip(jax.random.uniform(seeds[3], (KPOINTS, NB), jnp.float32, -4.0, 4.0) * block_levels(seeds[3], (KPOINTS, NB), ((0, 32),), -0.4, 0.0), -4.0, 4.0),
        "dipole": noise(seeds[4], (KPOINTS, 2 * NB * NB), 0.5, 3.0, ((0, 32),), jnp.float32),
        "pair_count": draw_pair_count(jax.random.fold_in(seeds[8], 71), 0),
        "pair_target": draw_pair_target(jax.random.fold_in(seeds[8], 71), 0),
        "kernel": noise(seeds[7], (NBLOCKS, MAXP * KB * KB), (4 * KB) ** -0.5, 1.0, (), jnp.float32),
    }


time_step = 0.1
pulse_amp = 3.0
pulse_center = 0.15
pulse_width = 0.2
pulse_freq = 2.0
highest = lax.Precision.HIGHEST


def pulse_field(moment):
    return pulse_amp * math.exp(-((moment - pulse_center) / pulse_width) ** 2) * math.cos(pulse_freq * moment)


def split_parts(flat_rows):
    pieces = flat_rows.reshape(flat_rows.shape[0], 2, NB, NB)
    return pieces[:, 0], pieces[:, 1]


def join_parts(real_part, imag_part):
    return jnp.stack([real_part, imag_part], axis=1).reshape(real_part.shape[0], 2 * NB * NB)


def hermitian(flat_rows):
    real_part, imag_part = split_parts(flat_rows)
    return join_parts(0.5 * (real_part + jnp.swapaxes(real_part, 1, 2)), 0.5 * (imag_part - jnp.swapaxes(imag_part, 1, 2)))


def band_tables():
    flat_index = jnp.arange(2 * NB * NB)
    channel = flat_index // (NB * NB)
    row_band = (flat_index // NB) % NB
    col_band = flat_index % NB
    on_diag = (channel == 0) & (row_band == col_band)
    ground = (on_diag & (row_band < NB // 2)).astype(jnp.float32)
    diag_table = (on_diag[None, :] & (row_band[None, :] == jnp.arange(NB)[:, None])).astype(jnp.float32)
    return ground, diag_table


def mat_prod(left_mat, right_mat):
    return jnp.einsum("kij,kjl->kil", left_mat, right_mat, precision=highest)


def change_of(hamilton, density_rows):
    ham_re, ham_im = split_parts(hamilton)
    rho_re, rho_im = split_parts(density_rows)
    comm_re = mat_prod(ham_re, rho_re) - mat_prod(ham_im, rho_im) - mat_prod(rho_re, ham_re) + mat_prod(rho_im, ham_im)
    comm_im = mat_prod(ham_re, rho_im) + mat_prod(ham_im, rho_re) - mat_prod(rho_re, ham_im) - mat_prod(rho_im, ham_re)
    return join_parts(comm_im, -comm_re)


def coupling_matrix(delta_rows):
    real_part, imag_part = split_parts(delta_rows)
    upper_rows = jnp.concatenate([real_part, -imag_part], axis=2)
    lower_rows = jnp.concatenate([imag_part, real_part], axis=2)
    return jnp.concatenate([upper_rows, lower_rows], axis=1)


def gram_to_rows(gram_sums):
    ham_re = gram_sums[:, :NB, :NB] + gram_sums[:, NB:, NB:]
    ham_im = gram_sums[:, :NB, NB:] - gram_sums[:, NB:, :NB]
    return join_parts(ham_re, ham_im)


def hartree_rows(delta_rows, bloch_blocks, coulomb):
    width_k = math.gcd(KPOINTS, 256)
    groups = KPOINTS // width_k
    matrices = coupling_matrix(delta_rows).reshape(groups, width_k, 2 * NB, 2 * NB)
    orbitals = bloch_blocks.reshape(groups, width_k, 2 * NB, NG)

    def density_part(inputs):
        matrix_rows, orbital_rows = inputs
        applied = jnp.einsum("kab,kbg->kag", matrix_rows, orbital_rows, precision=highest)
        return jnp.sum(orbital_rows * applied, axis=(0, 1))

    density = jnp.sum(lax.map(density_part, (matrices, orbitals)), axis=0)
    potential = coulomb * density / KPOINTS

    def gram_part(orbital_rows):
        return jnp.einsum("kag,kbg->kab", orbital_rows * potential, orbital_rows, precision=highest)

    gram_sums = lax.map(gram_part, orbitals).reshape(KPOINTS, 2 * NB, 2 * NB)
    return gram_to_rows(gram_sums)


def exchange_rows(delta_rows, pair_count, pair_target, kernel):
    blocks = delta_rows.reshape(NBLOCKS, KB, 2 * NB * NB)
    kernel_rows = kernel.reshape(NBLOCKS, MAXP, KB, KB)
    products = jnp.einsum("bpkl,blc->bpkc", kernel_rows, blocks, precision=highest)
    live_slot = (jnp.arange(MAXP)[None, :] < pair_count[:, None]).astype(jnp.float32)
    products = products * live_slot[:, :, None, None]
    summed = jnp.zeros((NBLOCKS, KB, 2 * NB * NB), jnp.float32)
    summed = summed.at[pair_target.reshape(NBLOCKS * MAXP)].add(products.reshape(NBLOCKS * MAXP, KB, 2 * NB * NB))
    return -summed.reshape(KPOINTS, 2 * NB * NB)


def reference(delta_rho, bloch_blocks, coulomb, energies, dipole, pair_count, pair_target, kernel):
    ground, diag_table = band_tables()
    band_diag = jnp.dot(energies, diag_table, precision=highest)
    dipole_h = hermitian(dipole)

    def hamiltonian(delta_rows, moment):
        hartree_part = hartree_rows(delta_rows, bloch_blocks, coulomb)
        sigma_part = exchange_rows(delta_rows, pair_count, pair_target, kernel)
        return band_diag + pulse_field(moment) * dipole_h + hartree_part + sigma_part

    current = hermitian(delta_rho)
    for step_number in range(STEPS):
        moment = step_number * time_step
        half_step = current + 0.5 * time_step * change_of(hamiltonian(current, moment), current + ground)
        current = current + time_step * change_of(hamiltonian(half_step, moment + 0.5 * time_step), half_step + ground)
    return current
```

```python
import functools
import math

import jax
import jax.numpy as jnp
import numpy as np
from jax import lax
from jax.experimental import pallas as pl
from jax.experimental.pallas import tpu as pltpu
from jax.sharding import PartitionSpec as P

NB = 8
KB = 8
MAXP = 8
STEPS = 3
NBLK = 8
NK = 64
NG = 1500
TILES = 12
WIDE = TILES * 128
CHIPS = 16
SIDE = 4
CHUNKS = 8

time_step = 0.1
pulse_amp = 3.0
pulse_center = 0.15
pulse_width = 0.2
pulse_freq = 2.0
highest = lax.Precision.HIGHEST
MESH = pl.DeviceIdType.MESH
f32 = jnp.float32

PLANE = [(a, b) for a in range(SIDE) for b in range(SIDE) if (a, b) != (0, 0)]


def pulse_field(moment):
    return (
        pulse_amp
        * math.exp(-(((moment - pulse_center) / pulse_width) ** 2))
        * math.cos(pulse_freq * moment)
    )


def component_tables():
    into = np.zeros((64, 128), np.float32)
    back = np.zeros((64, 128), np.float32)

    def real_entry(row, i, j):
        into[row, i * 8 + j] += 0.5
        into[row, j * 8 + i] += 0.5
        back[row, i * 8 + j] = 1.0
        back[row, j * 8 + i] = 1.0

    def imag_entry(row, i, j):
        into[row, 64 + i * 8 + j] += 0.5
        into[row, 64 + j * 8 + i] -= 0.5
        back[row, 64 + i * 8 + j] = 1.0
        back[row, 64 + j * 8 + i] = -1.0

    for i in range(8):
        real_entry(i, i, i)
        if i < 4:
            real_entry(8 + i, i, i + 4)
        else:
            imag_entry(8 + i, i, i - 4)
        for v in (1, 2, 3):
            real_entry(16 * v + i, i, (i + v) % 8)
            imag_entry(16 * v + 8 + i, i, (i + v) % 8)
    return into, back


def dot(a, b, lhs_dim, rhs_dim, precision=highest):
    return lax.dot_general(
        a, b, (((lhs_dim,), (rhs_dim,)), ((), ())), precision=precision, preferred_element_type=f32
    )


def iota(shape, axis):
    return lax.broadcasted_iota(jnp.int32, shape, axis)


def merge(a, b, bit):
    low = (iota((8, 128), 1) & (1 << bit)) == 0
    return jnp.where(low, a, b) + pltpu.roll(jnp.where(low, b, a), 1 << bit, 1)


def merge_all(values, bit):
    while len(values) > 1:
        values = [merge(a, b, bit) for a, b in zip(values[0::2], values[1::2])]
        bit += 1
    return values[0]


def rolled(value, up):
    up = up % 8
    return value if up == 0 else pltpu.roll(value, 8 - up, 0)


def swap(value):
    return pltpu.roll(value, 64, 1)


def offsets_of(packed):
    left = iota((8, 128), 1) < 64
    top = iota((8, 128), 0) < 4
    mixed_right = packed[0]
    mixed_left = swap(packed[0])
    zeroth = jnp.where(left, packed[0], 0.0)
    fourth = jnp.where(
        left,
        jnp.where(top, mixed_left, rolled(mixed_left, 4)),
        jnp.where(top, -rolled(mixed_right, 4), mixed_right),
    )
    diags = [zeroth, packed[1], packed[2], packed[3], fourth]
    for offset in (5, 6, 7):
        turned = rolled(diags[8 - offset], offset)
        diags.append(jnp.where(left, turned, -turned))
    return diags


def change_of(hamilton, state):
    left = iota((8, 128), 1) < 64
    top = iota((8, 128), 0) < 4
    ham = offsets_of(hamilton)
    rho = offsets_of(state)
    ham_swapped = [swap(h) for h in ham]
    ham_re = [jnp.where(left, h, s) for h, s in zip(ham, ham_swapped)]
    ham_im = [jnp.where(left, s, h) for h, s in zip(ham, ham_swapped)]
    products = []
    turned = [[rolled(rho[f], e) for e in range(8)] for f in range(8)]
    for d in range(8):
        from_re = None
        from_im = None
        for e in range(8):
            factor = turned[(d - e) % 8][e]
            term_re = ham_re[e] * factor
            from_re = term_re if e == 0 else from_re + term_re
            if e > 0:
                term_im = ham_im[e] * factor
                from_im = term_im if from_im is None else from_im + term_im
        crossed = swap(from_im)
        products.append(from_re + jnp.where(left, -crossed, crossed))
    changes = []
    for d in range(5):
        other = rolled(products[(8 - d) % 8], d)
        diff = products[d] - jnp.where(left, other, -other)
        crossed = swap(diff)
        changes.append(jnp.where(left, crossed, -crossed))
    mixed = jnp.where(top, swap(changes[4]), changes[4])
    return [jnp.where(left, changes[0], mixed)] + changes[1:4]


def kernel(
    rho_hbm, bloch_hbm, coulomb_hbm, energies_hbm, dipole_hbm, count_smem, target_hbm, kernel_hbm, into_hbm, back_hbm,
    out_ref,
    rho_buf, bands, coulomb_buf, energies_buf, dipole_buf, target_buf, kernel_buf, into_buf, back_buf,
    pairs, tail, partial, own_terms, couple, coulomb_rows,
    rho_send, rho_recv, core_send, core_recv, plane_send, plane_recv, sig_send, sig_recv, ham_recv,
    load_sem, band_sem, send_sem, recv_sem,
):
    ka = lax.axis_index("ka")
    ga = lax.axis_index("ga")
    core = lax.rem(ka, 2)
    chip = ka // 2
    chip_x = chip // SIDE
    chip_z = lax.rem(chip, SIDE)

    partner = (chip * 2 + (1 - core), ga)
    plane_chips = [
        lax.rem(chip_x + a, SIDE) * SIDE + lax.rem(chip_z + b, SIDE) for a, b in PLANE
    ]
    plane_ids = [(c * 2 + core, ga) for c in plane_chips]
    line_ids = [(ka, lax.rem(ga + d, SIDE)) for d in (1, 2, 3)]

    barrier = pltpu.get_barrier_semaphore()
    everyone = [partner] + plane_ids + line_ids
    for device in everyone:
        pl.semaphore_signal(barrier, inc=1, device_id=device, device_id_type=MESH)

    step_k = NK // CHUNKS
    band_loads = [
        pltpu.make_async_copy(
            bloch_hbm.at[pl.ds(n * step_k, step_k)],
            bands.at[pl.ds(n * step_k, step_k)],
            band_sem.at[n],
        )
        for n in range(CHUNKS)
    ]
    first_block = pl.multiple_of(chip * 16, 16)
    loads = [
        pltpu.make_async_copy(src, dst, load_sem.at[n])
        for n, (src, dst) in enumerate(
            [
                (rho_hbm, rho_buf),
                (into_hbm, into_buf),
                (dipole_hbm, dipole_buf),
                (energies_hbm, energies_buf),
                (coulomb_hbm, coulomb_buf),
                (target_hbm.at[pl.ds(first_block, 16)], target_buf),
                (kernel_hbm.at[pl.ds(first_block, 16)], kernel_buf),
                (back_hbm, back_buf),
            ]
        )
    ]
    for copy in loads:
        copy.start()
    for copy in band_loads:
        copy.start()

    lane = iota((8, 128), 1)
    row = iota((8, 128), 0)
    left = lane < 64
    top = row < 4

    tail[...] = jnp.zeros((NK, 2, 8, 128), f32)
    coulomb_rows[...] = jnp.zeros((16, 128), f32)

    for copy in loads:
        copy.wait()

    def packed_rows(rows):
        comps = dot(into_buf[...], jnp.concatenate([rows, rows], axis=0), 1, 1)
        return [
            jnp.where(left, comps[16 * v : 16 * v + 8], comps[16 * v + 8 : 16 * v + 16])
            for v in range(4)
        ]

    start = packed_rows(rho_buf[...])
    dipole_h = packed_rows(dipole_buf[...])
    unit = (iota((8, 8), 0) == iota((8, 8), 1)).astype(f32)
    level = dot(unit, jnp.concatenate([energies_buf[...]] * 2, axis=0), 1, 1)
    band_diag = jnp.where(left, level, 0.0)
    ground = jnp.where(left & top, 1.0, 0.0)

    for j in range(TILES):
        width = min(128, NG - j * 128)
        coulomb_rows[j : j + 1, 0:width] = coulomb_buf[0:1, j * 128 : j * 128 + width] * (1.0 / 2048.0)

    spread = (iota((8, 128), 1) // 16 == iota((8, 128), 0)).astype(f32)
    wide_target = dot(target_buf[...].astype(f32), spread, 1, 0)
    on_row = lax.rem(iota((16, 128), 1), 16) == iota((16, 128), 0)
    target_line = jnp.sum(jnp.where(on_row, wide_target, 0.0), axis=0, keepdims=True)
    lane_line = iota((1, 128), 1)
    count_line = jnp.zeros((1, 128), jnp.int32)
    for b in range(16):
        count_line = jnp.where(lax.rem(lane_line, 16) == b, count_smem[chip * 16 + b], count_line)
    live = lane_line // 16 < count_line
    wide_row = iota((128, 128), 0)
    wide_lane = iota((128, 128), 1)
    block_of_row = ((wide_row // 8) * 2 + core) * 8 + lax.rem(wide_row, 8)
    line = jnp.where(live, target_line, -1.0)
    hot = (line == block_of_row.astype(f32)).astype(f32)
    entry_rows = jnp.concatenate(
        [kernel_buf[:, p * 64 : (p + 1) * 64] for p in range(MAXP)], axis=0
    )
    for part in range(2):
        pick_row = iota((64, 128), 0)
        pick = (pick_row // 8 == 2 * ga + part) & (
            lax.rem(pick_row, 8) == lax.rem(iota((64, 128), 1), 8)
        )
        spread_rows = dot(entry_rows, pick.astype(f32), 1, 0)
        spread_rows = jnp.where(lax.rem(wide_row, 16) == wide_lane // 8, spread_rows, 0.0)
        couple[part] = -dot(hot, spread_rows, 1, 0)

    def build(k, _):
        last = (TILES - 1) * 128
        for part in range(2):
            tail[k, part, :, : NG - last] = bands[k, part, :, last:]
        for j in range(TILES):
            lanes = slice(j * 128, (j + 1) * 128)
            if j < TILES - 1:
                u, v = bands[k, 0, :, lanes], bands[k, 1, :, lanes]
            else:
                u, v = tail[k, 0], tail[k, 1]
            us = [u] + [rolled(u, d) for d in (1, 2, 3, 4)]
            vs = [v] + [rolled(v, d) for d in (1, 2, 3, 4)]
            values = [
                u * u + v * v,
                u * jnp.where(top, us[4], vs[4]) + v * jnp.where(top, vs[4], -us[4]),
            ]
            for d in (1, 2, 3):
                values += [u * us[d] + v * vs[d], u * vs[d] - v * us[d]]
            for t, value in enumerate(values):
                pairs[k * 8 + t, :, lanes] = value
        return 0

    for n, copy in enumerate(band_loads):
        copy.wait()
        lax.fori_loop(n * step_k, (n + 1) * step_k, build, 0)

    factors = [jnp.where(left, 1.0, jnp.where(top, 2.0, -2.0))] + [jnp.where(left, 2.0, -2.0)] * 3

    def density_of(state):
        weights = [f * s for f, s in zip(factors, state)]

        def add(step, sums):
            sums = list(sums)
            for r in range(2):
                k = step * 2 + r
                for half in range(2):
                    at = jnp.full((8, 128), half * 64 + k, jnp.int32)
                    for v in range(4):
                        weight = jnp.take_along_axis(weights[v], at, axis=1, mode="promise_in_bounds")
                        for j in range(TILES):
                            sums[j] = sums[j] + weight * pairs[k * 8 + 2 * v + half, :, j * 128 : (j + 1) * 128]
            return tuple(sums)

        zero = jnp.zeros((8, 128), f32)
        return lax.fori_loop(0, NK // 2, add, (zero,) * TILES)

    def gram_of(potential_rows):
        spread_v = [jnp.broadcast_to(potential_rows[j : j + 1], (8, 128)) for j in range(TILES)]

        def group(g, _):
            for t in range(8):
                sums = []
                for r in range(8):
                    k = g * 8 + r
                    total = None
                    for j in range(TILES):
                        term = spread_v[j] * pairs[k * 8 + t, :, j * 128 : (j + 1) * 128]
                        total = term if total is None else total + term
                    sums.append(total)
                partial[g * 8 + t] = merge_all(sums, 0)
            return 0

        lax.fori_loop(0, NK // 8, group, 0)
        packed = []
        for v in range(4):
            halves = [
                merge_all([partial[g * 8 + 2 * v + half] for g in range(8)], 3) for half in range(2)
            ]
            packed.append(merge(halves[0], halves[1], 6))
        return packed

    def remote(src, dst, send, recv, device):
        return pltpu.make_async_remote_copy(
            src_ref=src, dst_ref=dst, send_sem=send, recv_sem=recv, device_id=device, device_id_type=MESH
        )

    def wait_bytes(ref, sem):
        pltpu.make_async_copy(ref, ref, sem).wait()

    pl.semaphore_wait(barrier, len(everyone))

    def evaluate(e, carry):
        base, now = list(carry[:4]), list(carry[4:])
        par = lax.rem(e, 2)
        for v in range(4):
            rho_send[par, v] = now[v]
        to_partner = remote(
            rho_send.at[par], rho_recv.at[par], send_sem.at[0, par], recv_sem.at[0, par], partner
        )
        to_partner.start()

        sums = density_of(now)
        for j in range(TILES):
            core_send[par, j : j + 1] = jnp.sum(sums[j], axis=0, keepdims=True)
        core_copy = remote(
            core_send.at[par], core_recv.at[par], send_sem.at[1, par], recv_sem.at[1, par], partner
        )
        core_copy.start()
        core_copy.wait_recv()
        plane_send[par] = core_send[par] + core_recv[par]
        for n, device in enumerate(plane_ids):
            remote(
                plane_send.at[par], plane_recv.at[par, n], send_sem.at[2, par], recv_sem.at[2, par], device
            ).start()

        to_partner.wait_recv()
        rows = []
        for v in range(4):
            own = now[v]
            other = rho_recv[par, v]
            first = jnp.where(core == 0, own, other)
            second = jnp.where(core == 0, other, own)
            rows += [jnp.where(left, first, swap(second)), jnp.where(left, swap(first), second)]
        comps = jnp.concatenate(rows, axis=0)
        blank = jnp.zeros((64, 128), f32)
        messages = dot(couple[0], jnp.concatenate([comps, blank], axis=0), 1, 1)
        messages += dot(couple[1], jnp.concatenate([blank, comps], axis=0), 1, 1)
        for c in range(CHIPS):
            sig_send[par, c] = messages[c * 8 : (c + 1) * 8]
        for n, device in enumerate(plane_ids):
            remote(
                sig_send.at[par, plane_chips[n]],
                sig_recv.at[par, n],
                send_sem.at[3, par],
                recv_sem.at[3, par],
                device,
            ).start()

        wait_bytes(plane_recv.at[par], recv_sem.at[2, par])
        density = plane_send[par]
        for n in range(len(PLANE)):
            density = density + plane_recv[par, n]
        packed = gram_of(coulomb_rows[0:TILES] * density)

        wait_bytes(sig_recv.at[par], recv_sem.at[3, par])
        arrived = sig_send[par, chip]
        for n in range(len(PLANE)):
            arrived = arrived + sig_recv[par, n]
        place_row = iota((8, 128), 0)
        place_lane = lax.rem(iota((8, 128), 1), 64)
        for part in range(2):
            place = (place_lane == place_row * 8 + 2 * ga + part).astype(f32)
            sigma = dot(arrived, place, 0, 0)[part * 64 : part * 64 + 64]
            for v in range(4):
                packed[v] = packed[v] + jnp.where(
                    left, sigma[16 * v : 16 * v + 8], sigma[16 * v + 8 : 16 * v + 16]
                )
        for v in range(4):
            own_terms[par, v] = packed[v]
        for n, device in enumerate(line_ids):
            remote(
                own_terms.at[par], ham_recv.at[par, ga], send_sem.at[4, par], recv_sem.at[4 + n, par], device
            ).start()
        for v in range(4):
            ham_recv[par, ga, v] = packed[v]
        for n in range(3):
            source = lax.rem(ga + SIDE - (n + 1), SIDE)
            wait_bytes(ham_recv.at[par, source], recv_sem.at[4 + n, par])
        field = jnp.float32(0.0)
        for s in range(2 * STEPS):
            field = jnp.where(e == s, jnp.float32(pulse_field(0.5 * time_step * s)), field)
        ham = []
        for v in range(4):
            total = (ham_recv[par, 0, v] + ham_recv[par, 1, v]) + (ham_recv[par, 2, v] + ham_recv[par, 3, v])
            total = total + field * dipole_h[v]
            ham.append(total + band_diag if v == 0 else total)
        change = change_of(ham, [now[0] + ground] + now[1:])
        length = jnp.where(par == 0, jnp.float32(0.5 * time_step), jnp.float32(time_step))
        new = [b + length * c for b, c in zip(base, change)]
        base = [jnp.where(par == 0, b, n) for b, n in zip(base, new)]

        to_partner.wait_send()
        core_copy.wait_send()
        wait_bytes(plane_recv.at[par], send_sem.at[2, par])
        wait_bytes(sig_recv.at[par], send_sem.at[3, par])
        wait_bytes(ham_recv.at[par, pl.ds(0, 3)], send_sem.at[4, par])
        return tuple(base) + tuple(new)

    final = lax.fori_loop(0, 2 * STEPS, evaluate, tuple(start) + tuple(start))[:4]
    rows = []
    for v in range(4):
        rows += [final[v], swap(final[v])]
    out_ref[...] = dot(jnp.concatenate(rows, axis=0), back_buf[...], 0, 0)[:NK]


def local(delta_rho, bloch_blocks, coulomb, energies, dipole, pair_count, pair_target, kernel_list):
    into, back = component_tables()
    hbm = pl.BlockSpec(memory_space=pl.ANY)
    return pl.pallas_call(
        kernel,
        out_shape=jax.ShapeDtypeStruct((NK, 128), f32),
        in_specs=[hbm] * 5 + [pl.BlockSpec(memory_space=pltpu.SMEM)] + [hbm] * 4,
        out_specs=pl.BlockSpec(memory_space=pltpu.VMEM),
        scratch_shapes=[
            pltpu.VMEM((NK, 128), f32),
            pltpu.VMEM((NK, 2, NB, NG), f32),
            pltpu.VMEM((1, NG), f32),
            pltpu.VMEM((NK, NB), f32),
            pltpu.VMEM((NK, 128), f32),
            pltpu.VMEM((16, MAXP), jnp.int32),
            pltpu.VMEM((16, MAXP * KB * KB), f32),
            pltpu.VMEM((64, 128), f32),
            pltpu.VMEM((64, 128), f32),
            pltpu.VMEM((NK * 8, 8, WIDE), f32),
            pltpu.VMEM((NK, 2, 8, 128), f32),
            pltpu.VMEM((64, 8, 128), f32),
            pltpu.VMEM((2, 4, 8, 128), f32),
            pltpu.VMEM((2, 128, 128), f32),
            pltpu.VMEM((16, 128), f32),
            pltpu.VMEM((2, 4, 8, 128), f32),
            pltpu.VMEM((2, 4, 8, 128), f32),
            pltpu.VMEM((2, TILES, 128), f32),
            pltpu.VMEM((2, TILES, 128), f32),
            pltpu.VMEM((2, TILES, 128), f32),
            pltpu.VMEM((2, CHIPS - 1, TILES, 128), f32),
            pltpu.VMEM((2, CHIPS, 8, 128), f32),
            pltpu.VMEM((2, CHIPS - 1, 8, 128), f32),
            pltpu.VMEM((2, SIDE, 4, 8, 128), f32),
            pltpu.SemaphoreType.DMA((8,)),
            pltpu.SemaphoreType.DMA((CHUNKS,)),
            pltpu.SemaphoreType.DMA((5, 2)),
            pltpu.SemaphoreType.DMA((7, 2)),
        ],
        compiler_params=pltpu.CompilerParams(
            collective_id=0, has_side_effects=True, vmem_limit_bytes=52 * 1024 * 1024
        ),
        name="propagate",
    )(
        delta_rho,
        bloch_blocks,
        coulomb.reshape(1, NG),
        energies,
        dipole,
        pair_count,
        pair_target,
        kernel_list,
        jnp.asarray(into),
        jnp.asarray(back),
    )


def solution(mesh):
    in_specs = (
        P("ka", None),
        P("ka", None, None, "ga"),
        P("ga"),
        P("ka", None),
        P("ka", None),
        P(),
        P(),
        P(),
    )
    return jax.shard_map(local, mesh=mesh, in_specs=in_specs, out_specs=P("ka", None), check_vma=False)
```

```python
import functools
import math

import jax
import jax.numpy as jnp
import numpy as np
from jax import lax
from jax.experimental import pallas as pl
from jax.experimental.pallas import tpu as pltpu
from jax.sharding import PartitionSpec as P

NB = 8
KB = 8
MAXP = 8
STEPS = 3
NBLK = 8
NK = 64
NG = 1500
TILES = 12
WIDE = TILES * 128
CHIPS = 16
SIDE = 4
CHUNKS = 8
HALF = TILES // 2
UNROLL = 16

time_step = 0.1
pulse_amp = 3.0
pulse_center = 0.15
pulse_width = 0.2
pulse_freq = 2.0
highest = lax.Precision.HIGHEST
MESH = pl.DeviceIdType.MESH
f32 = jnp.float32


def hops(step):
    return min(step, SIDE - step)


PLANE = sorted(
    [(a, b) for a in range(SIDE) for b in range(SIDE) if (a, b) != (0, 0)],
    key=lambda at: -(hops(at[0]) + hops(at[1])),
)
LINE = (2, 1, 3)


def pulse_field(moment):
    return (
        pulse_amp
        * math.exp(-(((moment - pulse_center) / pulse_width) ** 2))
        * math.cos(pulse_freq * moment)
    )


def component_tables():
    into = np.zeros((64, 128), np.float32)
    back = np.zeros((64, 128), np.float32)

    def real_entry(row, i, j):
        into[row, i * 8 + j] += 0.5
        into[row, j * 8 + i] += 0.5
        back[row, i * 8 + j] = 1.0
        back[row, j * 8 + i] = 1.0

    def imag_entry(row, i, j):
        into[row, 64 + i * 8 + j] += 0.5
        into[row, 64 + j * 8 + i] -= 0.5
        back[row, 64 + i * 8 + j] = 1.0
        back[row, 64 + j * 8 + i] = -1.0

    for i in range(8):
        real_entry(i, i, i)
        if i < 4:
            real_entry(8 + i, i, i + 4)
        else:
            imag_entry(8 + i, i, i - 4)
        for v in (1, 2, 3):
            real_entry(16 * v + i, i, (i + v) % 8)
            imag_entry(16 * v + 8 + i, i, (i + v) % 8)
    return into, back


def dot(a, b, lhs_dim, rhs_dim, precision=highest):
    return lax.dot_general(
        a, b, (((lhs_dim,), (rhs_dim,)), ((), ())), precision=precision, preferred_element_type=f32
    )


def iota(shape, axis):
    return lax.broadcasted_iota(jnp.int32, shape, axis)


def rolled(value, up):
    up = up % 8
    return value if up == 0 else pltpu.roll(value, 8 - up, 0)


def swap(value):
    return pltpu.roll(value, 64, 1)


def unpacked(packed):
    left = iota((8, 128), 1) < 64
    comps = []
    for value in packed:
        other = swap(value)
        comps += [jnp.where(left, value, other), jnp.where(left, other, value)]
    return comps


def offsets_of(comps):
    top = iota((8, 128), 0) < 4
    mixed = comps[1]
    turned = rolled(mixed, 4)
    real = [comps[0], comps[2], comps[4], comps[6], jnp.where(top, mixed, turned)]
    imag = [None, comps[3], comps[5], comps[7], jnp.where(top, -turned, mixed)]
    for offset in (5, 6, 7):
        real.append(rolled(real[8 - offset], offset))
        imag.append(-rolled(imag[8 - offset], offset))
    return real, imag


def change_of(hamilton, state):
    top = iota((8, 128), 0) < 4
    ham_re, ham_im = offsets_of(hamilton)
    rho_re, rho_im = offsets_of(state)

    def add(total, term):
        return term if total is None else total + term

    prod_re, prod_im = [], []
    for d in range(8):
        plus, minus, cross = None, None, None
        for e in range(8):
            f = (d - e) % 8
            re = rolled(rho_re[f], e)
            plus = add(plus, ham_re[e] * re)
            if e > 0:
                cross = add(cross, ham_im[e] * re)
            if f > 0:
                im = rolled(rho_im[f], e)
                cross = add(cross, ham_re[e] * im)
                if e > 0:
                    minus = add(minus, ham_im[e] * im)
        prod_re.append(plus - minus)
        prod_im.append(cross)
    change_re, change_im = [], []
    for d in range(5):
        other = (8 - d) % 8
        change_re.append(prod_im[d] + rolled(prod_im[other], d))
        change_im.append(rolled(prod_re[other], d) - prod_re[d])
    return [
        change_re[0],
        jnp.where(top, change_re[4], change_im[4]),
        change_re[1],
        change_im[1],
        change_re[2],
        change_im[2],
        change_re[3],
        change_im[3],
    ]


def build_pairs(bands, tail, pairs, first, last):
    top = iota((8, 128), 0) < 4

    def build(k, _):
        edge = (TILES - 1) * 128
        for part in range(2):
            tail[k, part, :, : NG - edge] = bands[k, part, :, edge:]
        for j in range(TILES):
            lanes = slice(j * 128, (j + 1) * 128)
            if j < TILES - 1:
                u, v = bands[k, 0, :, lanes], bands[k, 1, :, lanes]
            else:
                u, v = tail[k, 0], tail[k, 1]
            us = [u] + [rolled(u, d) for d in (1, 2, 3, 4)]
            vs = [v] + [rolled(v, d) for d in (1, 2, 3, 4)]
            values = [
                u * u + v * v,
                u * jnp.where(top, us[4], vs[4]) + v * jnp.where(top, vs[4], -us[4]),
            ]
            for d in (1, 2, 3):
                values += [u * us[d] + v * vs[d], u * vs[d] - v * us[d]]
            for t, value in enumerate(values):
                pairs[k * 8 + t, :, lanes] = value
        return 0

    lax.fori_loop(first, last, build, 0)


def density_of(pairs, state, first):
    top = iota((8, 128), 0) < 4
    weights = [state[0], jnp.where(top, 2.0, -2.0) * state[1]]
    for v in (1, 2, 3):
        weights += [2.0 * state[2 * v], -2.0 * state[2 * v + 1]]

    def add(step, sums):
        sums = list(sums)
        for r in range(UNROLL):
            k = step * UNROLL + r
            at = jnp.full((8, 128), k, jnp.int32)
            for t in range(8):
                weight = jnp.take_along_axis(weights[t], at, axis=1, mode="promise_in_bounds")
                for j in range(HALF):
                    lanes = slice((first + j) * 128, (first + j + 1) * 128)
                    sums[j] = sums[j] + weight * pairs[k * 8 + t, :, lanes]
        return tuple(sums)

    return lax.fori_loop(0, NK // UNROLL, add, (jnp.zeros((8, 128), f32),) * HALF)


def gram_of(pairs, rows, first):
    lane = iota((8, 128), 1)
    spread = [jnp.broadcast_to(rows[j : j + 1], (8, 128)) for j in range(HALF)]

    def group(step, packed):
        packed = list(packed)
        for r in range(UNROLL):
            k = step * UNROLL + r
            for t in range(8):
                total = None
                for j in range(HALF):
                    lanes = slice((first + j) * 128, (first + j + 1) * 128)
                    term = spread[j] * pairs[k * 8 + t, :, lanes]
                    total = term if total is None else total + term
                summed = jnp.broadcast_to(jnp.sum(total, axis=1, keepdims=True), (8, 128))
                packed[t // 2] = jnp.where(lane == (t % 2) * 64 + k, summed, packed[t // 2])
        return tuple(packed)

    return lax.fori_loop(0, NK // UNROLL, group, (jnp.zeros((8, 128), f32),) * 4)


def kernel(
    rho_hbm, bloch_hbm, coulomb_hbm, energies_hbm, dipole_hbm, count_hbm, target_hbm, kernel_hbm, into_hbm, back_hbm,
    out_ref,
    rho_buf, bands, coulomb_buf, energies_buf, dipole_buf, count_buf, target_buf, kernel_buf, into_buf, back_buf,
    pairs, tail, couple, coulomb_rows,
    rho_send, rho_recv, core_send, core_recv, plane_send, plane_recv, sig_send, sig_recv, rows_send, rows_recv,
    ham_send, ham_recv,
    load_sem, band_sem, send_sem, recv_sem,
):
    ka = lax.axis_index("ka")
    ga = lax.axis_index("ga")
    core = lax.rem(ka, 2)
    chip = ka // 2
    chip_x = chip // SIDE
    chip_z = lax.rem(chip, SIDE)

    partner = (chip * 2 + (1 - core), ga)
    plane_chips = [
        lax.rem(chip_x + a, SIDE) * SIDE + lax.rem(chip_z + b, SIDE) for a, b in PLANE
    ]
    plane_ids = [(c * 2 + core, ga) for c in plane_chips]
    line_ids = [(ka, lax.rem(ga + d, SIDE)) for d in LINE]
    line_sources = [lax.rem(ga + SIDE - d, SIDE) for d in LINE]

    barrier = pltpu.get_barrier_semaphore()
    everyone = [partner] + plane_ids + line_ids
    for device in everyone:
        pl.semaphore_signal(barrier, inc=1, device_id=device, device_id_type=MESH)

    step_k = NK // CHUNKS
    band_loads = [
        pltpu.make_async_copy(
            bloch_hbm.at[pl.ds(n * step_k, step_k)],
            bands.at[pl.ds(n * step_k, step_k)],
            band_sem.at[n],
        )
        for n in range(CHUNKS)
    ]
    first_block = pl.multiple_of(chip * 16, 16)
    loads = [
        pltpu.make_async_copy(src, dst, load_sem.at[n])
        for n, (src, dst) in enumerate(
            [
                (rho_hbm, rho_buf),
                (into_hbm, into_buf),
                (dipole_hbm, dipole_buf),
                (energies_hbm, energies_buf),
                (coulomb_hbm, coulomb_buf),
                (count_hbm, count_buf),
                (target_hbm, target_buf),
                (kernel_hbm.at[pl.ds(first_block, 16)], kernel_buf),
                (back_hbm, back_buf),
            ]
        )
    ]
    for copy in loads:
        copy.start()
    for copy in band_loads:
        copy.start()

    lane = iota((8, 128), 1)
    row = iota((8, 128), 0)
    left = lane < 64
    top = row < 4

    tail[...] = jnp.zeros((NK, 2, 8, 128), f32)
    coulomb_rows[...] = jnp.zeros((2, 8, 128), f32)
    core_send[...] = jnp.zeros((2, 2, 8, 128), f32)

    for copy in loads:
        copy.wait()

    def components(rows):
        comps = dot(into_buf[...], jnp.concatenate([rows, rows], axis=0), 1, 1)
        return [comps[8 * t : 8 * t + 8] for t in range(8)]

    start = components(rho_buf[...])
    dipole_h = components(dipole_buf[...])
    band_diag = jnp.concatenate([energies_buf[...]] * 2, axis=1)
    ground = jnp.where(top, 1.0, 0.0)

    for j in range(TILES):
        width = min(128, NG - j * 128)
        coulomb_rows[j // HALF, j % HALF : j % HALF + 1, 0:width] = (
            coulomb_buf[j * 128 : j * 128 + width].reshape(1, width) * (1.0 / 2048.0)
        )

    chosen = (iota((256, 128), 0) == chip * 16 + lax.rem(iota((256, 128), 1), 16)).astype(f32)
    wide_target = dot(target_buf[...].astype(f32), chosen, 1, 0)
    target_line = jnp.sum(jnp.where(lane // 16 == row, wide_target, 0.0), axis=0, keepdims=True)
    counts = jnp.broadcast_to(count_buf[...].astype(f32).reshape(1, 256), (8, 256))
    live = (iota((1, 128), 1) // 16).astype(f32) < dot(counts, chosen, 1, 0)[0:1]
    wide_row = iota((128, 128), 0)
    wide_lane = iota((128, 128), 1)
    block_of_row = ((wide_row // 8) * 2 + core) * 8 + lax.rem(wide_row, 8)
    line = jnp.where(live, target_line, -1.0)
    hot = (line == block_of_row.astype(f32)).astype(f32)
    entry_rows = jnp.concatenate(
        [kernel_buf[:, p * 64 : (p + 1) * 64] for p in range(MAXP)], axis=0
    )
    for part in range(2):
        pick_row = iota((64, 128), 0)
        pick = (pick_row // 8 == 2 * ga + part) & (
            lax.rem(pick_row, 8) == lax.rem(iota((64, 128), 1), 8)
        )
        spread_rows = dot(entry_rows, pick.astype(f32), 1, 0)
        spread_rows = jnp.where(lax.rem(wide_row, 16) == wide_lane // 8, spread_rows, 0.0)
        couple[part] = -dot(hot, spread_rows, 1, 0)

    for n, copy in enumerate(band_loads):
        copy.wait()
        build_pairs(bands, tail, pairs, n * step_k, (n + 1) * step_k)

    def remote(src, dst, send, recv, device):
        return pltpu.make_async_remote_copy(
            src_ref=src, dst_ref=dst, send_sem=send, recv_sem=recv, device_id=device, device_id_type=MESH
        )

    def wait_bytes(ref, sem):
        pltpu.make_async_copy(ref, ref, sem).wait()

    pl.semaphore_wait(barrier, len(everyone))

    def evaluate(e, carry):
        base, now = list(carry[:8]), list(carry[8:])
        par = lax.rem(e, 2)
        for v in range(4):
            rho_send[par, v] = jnp.where(left, now[2 * v], now[2 * v + 1])
        to_partner = remote(
            rho_send.at[par], rho_recv.at[par], send_sem.at[0, par], recv_sem.at[0, par], partner
        )
        to_partner.start()

        core_copies = []
        for half in range(2):
            sums = density_of(pairs, now, half * HALF)
            for j in range(HALF):
                core_send[par, half, j : j + 1] = jnp.sum(sums[j], axis=0, keepdims=True)
            core_copies.append(
                remote(
                    core_send.at[par, half],
                    core_recv.at[par, half],
                    send_sem.at[1 + half, par],
                    recv_sem.at[1 + half, par],
                    partner,
                )
            )
            core_copies[half].start()

        def to_plane(half):
            core_copies[half].wait_recv()
            plane_send[par, half] = core_send[par, half] + core_recv[par, half]
            for n, device in enumerate(plane_ids):
                remote(
                    plane_send.at[par, half],
                    plane_recv.at[par, half, n],
                    send_sem.at[3 + half, par],
                    recv_sem.at[3 + half, par],
                    device,
                ).start()

        to_plane(0)

        to_partner.wait_recv()
        others = unpacked([rho_recv[par, v] for v in range(4)])
        first_core = core == 0
        rows = []
        for t in range(8):
            first = jnp.where(first_core, now[t], others[t])
            second = jnp.where(first_core, others[t], now[t])
            rows.append(jnp.where(left, first, second))
        comps = jnp.concatenate(rows, axis=0)
        blank = jnp.zeros((64, 128), f32)
        messages = dot(couple[0], jnp.concatenate([comps, blank], axis=0), 1, 1)
        messages += dot(couple[1], jnp.concatenate([blank, comps], axis=0), 1, 1)
        for c in range(CHIPS):
            sig_send[par, c] = messages[c * 8 : (c + 1) * 8]
        for n, device in enumerate(plane_ids):
            remote(
                sig_send.at[par, plane_chips[n]],
                sig_recv.at[par, n],
                send_sem.at[5, par],
                recv_sem.at[5, par],
                device,
            ).start()

        to_plane(1)

        def potential_of(half):
            wait_bytes(plane_recv.at[par, half], recv_sem.at[3 + half, par])
            density = plane_send[par, half]
            for n in range(len(PLANE)):
                density = density + plane_recv[par, half, n]
            return coulomb_rows[half] * density

        packed = gram_of(pairs, potential_of(0), 0)

        wait_bytes(sig_recv.at[par], recv_sem.at[5, par])
        arrived = sig_send[par, chip]
        for n in range(len(PLANE)):
            arrived = arrived + sig_recv[par, n]
        rows_send[par] = arrived
        for n, device in enumerate(line_ids):
            remote(
                rows_send.at[par], rows_recv.at[par, ga], send_sem.at[6, par], recv_sem.at[6 + n, par], device
            ).start()
        rows_recv[par, ga] = arrived

        second = gram_of(pairs, potential_of(1), HALF)
        packed = [a + b for a, b in zip(packed, second)]
        for v in range(4):
            ham_send[par, v] = packed[v]
        for n, device in enumerate(line_ids):
            remote(
                ham_send.at[par], ham_recv.at[par, ga], send_sem.at[7, par], recv_sem.at[9 + n, par], device
            ).start()
        for v in range(4):
            ham_recv[par, ga, v] = packed[v]

        for n, source in enumerate(line_sources):
            wait_bytes(rows_recv.at[par, source], recv_sem.at[6 + n, par])
        all_rows = jnp.concatenate([rows_recv[par, g] for g in range(SIDE)], axis=0)
        place_row = iota((32, 128), 0)
        place_lane = lax.rem(iota((32, 128), 1), 64)
        sigma = None
        for part in range(2):
            at = lax.rem(place_row, 8) * 8 + 2 * (place_row // 8) + part
            placed = dot(all_rows, (place_lane == at).astype(f32), 0, 0)[part * 64 : part * 64 + 64]
            sigma = placed if sigma is None else sigma + placed
        field = jnp.float32(0.0)
        for s in range(2 * STEPS):
            field = jnp.where(e == s, jnp.float32(pulse_field(0.5 * time_step * s)), field)
        known = [sigma[8 * t : 8 * t + 8] + field * dipole_h[t] for t in range(8)]
        known[0] = known[0] + band_diag

        for n, source in enumerate(line_sources):
            wait_bytes(ham_recv.at[par, source], recv_sem.at[9 + n, par])
        hartree = unpacked(
            [
                (ham_recv[par, 0, v] + ham_recv[par, 1, v]) + (ham_recv[par, 2, v] + ham_recv[par, 3, v])
                for v in range(4)
            ]
        )
        ham = [h + other for h, other in zip(hartree, known)]
        change = change_of(ham, [now[0] + ground] + now[1:])
        length = jnp.where(par == 0, jnp.float32(0.5 * time_step), jnp.float32(time_step))
        new = [b + length * c for b, c in zip(base, change)]
        base = [jnp.where(par == 0, b, n) for b, n in zip(base, new)]

        to_partner.wait_send()
        for half in range(2):
            core_copies[half].wait_send()
            wait_bytes(plane_recv.at[par, half], send_sem.at[3 + half, par])
        wait_bytes(sig_recv.at[par], send_sem.at[5, par])
        wait_bytes(rows_recv.at[par, pl.ds(0, 3)], send_sem.at[6, par])
        wait_bytes(ham_recv.at[par, pl.ds(0, 3)], send_sem.at[7, par])
        return tuple(base) + tuple(new)

    final = lax.fori_loop(0, 2 * STEPS, evaluate, tuple(start) + tuple(start))[:8]
    out_ref[...] = dot(jnp.concatenate(final, axis=0), back_buf[...], 0, 0)[:NK]


def local(delta_rho, bloch_blocks, coulomb, energies, dipole, pair_count, pair_target, kernel_list):
    into, back = component_tables()
    hbm = pl.BlockSpec(memory_space=pltpu.HBM)
    return pl.pallas_call(
        kernel,
        out_shape=jax.ShapeDtypeStruct((NK, 128), f32),
        in_specs=[hbm] * 10,
        out_specs=pl.BlockSpec(memory_space=pltpu.VMEM),
        scratch_shapes=[
            pltpu.VMEM((NK, 128), f32),
            pltpu.VMEM((NK, 2, NB, NG), f32),
            pltpu.VMEM((NG,), f32),
            pltpu.VMEM((NB, NK), f32),
            pltpu.VMEM((NK, 128), f32),
            pltpu.VMEM((256,), jnp.int32),
            pltpu.VMEM((MAXP, 256), jnp.int32),
            pltpu.VMEM((16, MAXP * KB * KB), f32),
            pltpu.VMEM((64, 128), f32),
            pltpu.VMEM((64, 128), f32),
            pltpu.VMEM((NK * 8, 8, WIDE), f32),
            pltpu.VMEM((NK, 2, 8, 128), f32),
            pltpu.VMEM((2, 128, 128), f32),
            pltpu.VMEM((2, 8, 128), f32),
            pltpu.VMEM((2, 4, 8, 128), f32),
            pltpu.VMEM((2, 4, 8, 128), f32),
            pltpu.VMEM((2, 2, 8, 128), f32),
            pltpu.VMEM((2, 2, 8, 128), f32),
            pltpu.VMEM((2, 2, 8, 128), f32),
            pltpu.VMEM((2, 2, CHIPS - 1, 8, 128), f32),
            pltpu.VMEM((2, CHIPS, 8, 128), f32),
            pltpu.VMEM((2, CHIPS - 1, 8, 128), f32),
            pltpu.VMEM((2, 8, 128), f32),
            pltpu.VMEM((2, SIDE, 8, 128), f32),
            pltpu.VMEM((2, 4, 8, 128), f32),
            pltpu.VMEM((2, SIDE, 4, 8, 128), f32),
            pltpu.SemaphoreType.DMA((9,)),
            pltpu.SemaphoreType.DMA((CHUNKS,)),
            pltpu.SemaphoreType.DMA((8, 2)),
            pltpu.SemaphoreType.DMA((12, 2)),
        ],
        compiler_params=pltpu.CompilerParams(
            collective_id=0, has_side_effects=True, vmem_limit_bytes=58 * 1024 * 1024
        ),
        name="propagate",
    )(
        delta_rho,
        bloch_blocks,
        coulomb,
        energies.T,
        dipole,
        pair_count,
        pair_target.T,
        kernel_list,
        jnp.asarray(into),
        jnp.asarray(back),
    )


def solution(mesh):
    in_specs = (
        P("ka", None),
        P("ka", None, None, "ga"),
        P("ga"),
        P("ka", None),
        P("ka", None),
        P(),
        P(),
        P(),
    )
    return jax.shard_map(local, mesh=mesh, in_specs=in_specs, out_specs=P("ka", None), check_vma=False)
```

```python
import functools
import math

import jax
import jax.numpy as jnp
import numpy as np
from jax import lax
from jax.experimental import pallas as pl
from jax.experimental.pallas import tpu as pltpu
from jax.sharding import PartitionSpec as P

NB = 8
KB = 8
MAXP = 8
STEPS = 3
NBLK = 8
NK = 64
NG = 1500
TILES = 12
SIDE = 4
CHUNKS = 8
HALF = TILES // 2
UNROLL = 64

time_step = 0.1
pulse_amp = 3.0
pulse_center = 0.15
pulse_width = 0.2
pulse_freq = 2.0
highest = lax.Precision.HIGHEST
MESH = pl.DeviceIdType.MESH
f32 = jnp.float32


def hops(step):
    return min(step, SIDE - step)


LAYER = [(a, b, c) for a in range(SIDE) for b in range(SIDE) for c in range(2)]
DEVICES = len(LAYER)
ORDER = sorted(range(1, DEVICES), key=lambda n: -(hops(LAYER[n][0]) + hops(LAYER[n][1])))
LINE = (2, 1, 3)


def pulse_field(moment):
    return (
        pulse_amp
        * math.exp(-(((moment - pulse_center) / pulse_width) ** 2))
        * math.cos(pulse_freq * moment)
    )


def component_tables():
    into = np.zeros((64, 128), np.float32)
    back = np.zeros((64, 128), np.float32)

    def real_entry(row, i, j):
        into[row, i * 8 + j] += 0.5
        into[row, j * 8 + i] += 0.5
        back[row, i * 8 + j] = 1.0
        back[row, j * 8 + i] = 1.0

    def imag_entry(row, i, j):
        into[row, 64 + i * 8 + j] += 0.5
        into[row, 64 + j * 8 + i] -= 0.5
        back[row, 64 + i * 8 + j] = 1.0
        back[row, 64 + j * 8 + i] = -1.0

    for i in range(8):
        real_entry(i, i, i)
        if i < 4:
            real_entry(8 + i, i, i + 4)
        else:
            imag_entry(8 + i, i, i - 4)
        for v in (1, 2, 3):
            real_entry(16 * v + i, i, (i + v) % 8)
            imag_entry(16 * v + 8 + i, i, (i + v) % 8)
    return into, back


def dot(a, b, lhs_dim, rhs_dim, precision=highest):
    return lax.dot_general(
        a, b, (((lhs_dim,), (rhs_dim,)), ((), ())), precision=precision, preferred_element_type=f32
    )


def iota(shape, axis):
    return lax.broadcasted_iota(jnp.int32, shape, axis)


def rolled(value, up):
    up = up % 8
    return value if up == 0 else pltpu.roll(value, 8 - up, 0)


def swap(value):
    return pltpu.roll(value, 64, 1)


def unpacked(packed):
    left = iota((8, 128), 1) < 64
    comps = []
    for value in packed:
        other = swap(value)
        comps += [jnp.where(left, value, other), jnp.where(left, other, value)]
    return comps


def offsets_of(comps):
    top = iota((8, 128), 0) < 4
    mixed = comps[1]
    turned = rolled(mixed, 4)
    real = [comps[0], comps[2], comps[4], comps[6], jnp.where(top, mixed, turned)]
    imag = [None, comps[3], comps[5], comps[7], jnp.where(top, -turned, mixed)]
    for offset in (5, 6, 7):
        real.append(rolled(real[8 - offset], offset))
        imag.append(-rolled(imag[8 - offset], offset))
    return real, imag


def change_of(hamilton, state):
    top = iota((8, 128), 0) < 4
    ham_re, ham_im = offsets_of(hamilton)
    rho_re, rho_im = offsets_of(state)

    def add(total, term):
        return term if total is None else total + term

    prod_re, prod_im = [], []
    for d in range(8):
        plus, minus, cross = None, None, None
        for e in range(8):
            f = (d - e) % 8
            re = rolled(rho_re[f], e)
            plus = add(plus, ham_re[e] * re)
            if e > 0:
                cross = add(cross, ham_im[e] * re)
            if f > 0:
                im = rolled(rho_im[f], e)
                cross = add(cross, ham_re[e] * im)
                if e > 0:
                    minus = add(minus, ham_im[e] * im)
        prod_re.append(plus - minus)
        prod_im.append(cross)
    change_re, change_im = [], []
    for d in range(5):
        other = (8 - d) % 8
        change_re.append(prod_im[d] + rolled(prod_im[other], d))
        change_im.append(rolled(prod_re[other], d) - prod_re[d])
    return [
        change_re[0],
        jnp.where(top, change_re[4], change_im[4]),
        change_re[1],
        change_im[1],
        change_re[2],
        change_im[2],
        change_re[3],
        change_im[3],
    ]


def build_pairs(bands, tail, pairs, first, last):
    top = iota((8, 128), 0) < 4

    def build(k, _):
        edge = (TILES - 1) * 128
        for part in range(2):
            tail[k, part, :, : NG - edge] = bands[k, part, :, edge:]
        for j in range(TILES):
            lanes = slice(j * 128, (j + 1) * 128)
            if j < TILES - 1:
                u, v = bands[k, 0, :, lanes], bands[k, 1, :, lanes]
            else:
                u, v = tail[k, 0], tail[k, 1]
            us = [u] + [rolled(u, d) for d in (1, 2, 3, 4)]
            vs = [v] + [rolled(v, d) for d in (1, 2, 3, 4)]
            values = [
                u * u + v * v,
                u * jnp.where(top, us[4], vs[4]) + v * jnp.where(top, vs[4], -us[4]),
            ]
            for d in (1, 2, 3):
                values += [u * us[d] + v * vs[d], u * vs[d] - v * us[d]]
            for t, value in enumerate(values):
                pairs[j // HALF, k * 8 + t, :, (j % HALF) * 128 : (j % HALF + 1) * 128] = value
        return 0

    lax.fori_loop(first, last, build, 0)


def loop(body, carry):
    return body(0, carry) if UNROLL == NK else lax.fori_loop(0, NK // UNROLL, body, carry)


def density_of(pairs, state, half):
    top = iota((8, 128), 0) < 4
    weights = [state[0], jnp.where(top, 2.0, -2.0) * state[1]]
    for v in (1, 2, 3):
        weights += [2.0 * state[2 * v], -2.0 * state[2 * v + 1]]

    def add(step, sums):
        sums = list(sums)
        for r in range(UNROLL):
            k = step * UNROLL + r
            at = jnp.full((8, 128), k, jnp.int32)
            for t in range(8):
                weight = jnp.take_along_axis(weights[t], at, axis=1, mode="promise_in_bounds")
                for j in range(HALF):
                    sums[j] = sums[j] + weight * pairs[half, k * 8 + t, :, j * 128 : (j + 1) * 128]
        return tuple(sums)

    return loop(add, (jnp.zeros((8, 128), f32),) * HALF)


def gram_of(pairs, rows, half):
    lane = iota((8, 128), 1)
    spread = [jnp.broadcast_to(rows[j : j + 1], (8, 128)) for j in range(HALF)]

    def group(step, packed):
        packed = list(packed)
        for r in range(UNROLL):
            k = step * UNROLL + r
            for t in range(8):
                total = None
                for j in range(HALF):
                    term = spread[j] * pairs[half, k * 8 + t, :, j * 128 : (j + 1) * 128]
                    total = term if total is None else total + term
                summed = jnp.broadcast_to(jnp.sum(total, axis=1, keepdims=True), (8, 128))
                packed[t // 2] = jnp.where(lane == (t % 2) * 64 + k, summed, packed[t // 2])
        return tuple(packed)

    return loop(group, (jnp.zeros((8, 128), f32),) * 4)


def kernel(
    rho_hbm, bloch_hbm, coulomb_hbm, energies_hbm, dipole_hbm, count_hbm, target_hbm, kernel_hbm, into_hbm, back_hbm,
    out_ref,
    rho_buf, bands, coulomb_buf, energies_buf, dipole_buf, count_buf, target_buf, kernel_buf, into_buf, back_buf,
    pairs, tail, couple, coulomb_rows,
    place, first_send, first_recv, second_send, second_recv, rows_send, rows_recv,
    ham_send, ham_recv,
    load_sem, band_sem, send_sem, recv_sem,
):
    ka = lax.axis_index("ka")
    ga = lax.axis_index("ga")
    core = lax.rem(ka, 2)
    chip = ka // 2
    chip_x = chip // SIDE
    chip_z = lax.rem(chip, SIDE)

    def layer_device(a, b, c):
        return (lax.rem(chip_x + a, SIDE) * SIDE + lax.rem(chip_z + b, SIDE)) * 2 + lax.rem(core + c, 2)

    layer_ids = [(layer_device(*offset), ga) for offset in LAYER]
    line_ids = [(ka, lax.rem(ga + d, SIDE)) for d in LINE]
    line_sources = [lax.rem(ga + SIDE - d, SIDE) for d in LINE]

    barrier = pltpu.get_barrier_semaphore()
    everyone = layer_ids[1:] + line_ids
    for device in everyone:
        pl.semaphore_signal(barrier, inc=1, device_id=device, device_id_type=MESH)

    step_k = NK // CHUNKS
    band_loads = [
        pltpu.make_async_copy(
            bloch_hbm.at[pl.ds(n * step_k, step_k)],
            bands.at[pl.ds(n * step_k, step_k)],
            band_sem.at[n],
        )
        for n in range(CHUNKS)
    ]
    first_block = pl.multiple_of(ka * NBLK, NBLK)
    loads = [
        pltpu.make_async_copy(src, dst, load_sem.at[n])
        for n, (src, dst) in enumerate(
            [
                (rho_hbm, rho_buf),
                (into_hbm, into_buf),
                (dipole_hbm, dipole_buf),
                (energies_hbm, energies_buf),
                (coulomb_hbm, coulomb_buf),
                (count_hbm, count_buf),
                (target_hbm, target_buf),
                (kernel_hbm.at[pl.ds(first_block, NBLK)], kernel_buf),
                (back_hbm, back_buf),
            ]
        )
    ]
    for copy in loads:
        copy.start()
    for copy in band_loads:
        copy.start()

    lane = iota((8, 128), 1)
    row = iota((8, 128), 0)
    left = lane < 64
    top = row < 4

    tail[...] = jnp.zeros((NK, 2, 8, 128), f32)
    coulomb_rows[...] = jnp.zeros((2, 8, 128), f32)

    for copy in loads:
        copy.wait()

    def components(rows):
        comps = dot(into_buf[...], jnp.concatenate([rows, rows], axis=0), 1, 1)
        return [comps[8 * t : 8 * t + 8] for t in range(8)]

    start = components(rho_buf[...])
    dipole_h = components(dipole_buf[...])
    band_diag = jnp.concatenate([energies_buf[...]] * 2, axis=1)
    ground = jnp.where(top, 1.0, 0.0)

    for j in range(TILES):
        width = min(128, NG - j * 128)
        coulomb_rows[j // HALF, j % HALF : j % HALF + 1, 0:width] = (
            coulomb_buf[j * 128 : j * 128 + width].reshape(1, width) * (1.0 / 2048.0)
        )

    def exact(a, b, lhs_dim, rhs_dim):
        return dot(a.astype(f32), b.astype(f32), lhs_dim, rhs_dim)

    target = target_buf[...]
    blocks = iota((8, 256), 1)
    counts = jnp.broadcast_to(count_buf[...].reshape(1, 256), (8, 256))
    live = iota((8, 256), 0) < counts
    wide_row = iota((256, 256), 0)
    wide_lane = iota((256, 256), 1)
    same = wide_row // 8 == wide_lane // 8
    before = same & (wide_row < wide_lane)
    lower = iota((8, 8), 1) < iota((8, 8), 0)

    own_block = (iota((256, 128), 0) == ka * 8 + lax.rem(iota((256, 128), 1), 8)) & (iota((256, 128), 1) < 64)
    on_p = row == lane // 8
    line = jnp.sum(
        jnp.where(on_p, exact(jnp.where(live, target // 8, -1), own_block, 1, 0), 0.0), axis=0, keepdims=True
    )
    square_row = iota((128, 128), 0)
    square_lane = iota((128, 128), 1)
    square = jnp.broadcast_to(line, (128, 128))
    column = jnp.sum(jnp.where(square_row == square_lane, square, 0.0), axis=1, keepdims=True)
    rank = jnp.sum(
        jnp.where((column == square) & (square_row < square_lane), 1.0, 0.0), axis=0, keepdims=True
    )
    to = iota((256, 128), 0) // 8
    to_device = (
        lax.rem(chip_x + to // 8, SIDE) * SIDE + lax.rem(chip_z + lax.rem(to // 2, SIDE), SIDE)
    ) * 2 + lax.rem(core + lax.rem(to, 2), 2)
    slot = (lax.rem(iota((256, 128), 0), 8) - HALF).astype(f32)
    hot = (line == to_device.astype(f32)) & (rank == slot) & (iota((256, 128), 1) < 64)
    entry_rows = jnp.concatenate(
        [kernel_buf[:, p * 64 : (p + 1) * 64] for p in range(MAXP)] + [jnp.zeros((64, 64), f32)], axis=0
    )
    for part in range(2):
        pick_row = iota((64, 128), 0)
        pick = (pick_row // 8 == 2 * ga + part) & (
            lax.rem(pick_row, 8) == lax.rem(iota((64, 128), 1), 8)
        )
        spread_rows = exact(entry_rows, pick, 1, 0)
        keep = (lax.rem(square_row, 8) == square_lane // 8) & (square_lane < 64)
        couple[part] = -exact(hot, jnp.where(keep, spread_rows, 0.0), 1, 0)

    mine = live & (target // 8 == ka)
    mine_f = mine.astype(f32)
    ranks = exact(mine, before, 1, 0) + exact(exact(lower, mine, 1, 0), same, 1, 0)
    source = wide_lane // 8
    source_device = (
        lax.rem(chip_x + SIDE - source // 8, SIDE) * SIDE + lax.rem(chip_z + SIDE - lax.rem(source // 2, SIDE), SIDE)
    ) * 2 + lax.rem(core + lax.rem(source, 2), 2)
    placed = jnp.zeros((8, 256), f32)
    for number in range(2):
        of_slot = jnp.where(ranks == number, mine_f, 0.0)
        by_block = jnp.zeros((8, 256), f32)
        for q in range(8):
            found = jnp.sum(jnp.where(lax.rem(target, 8) == q, of_slot, 0.0), axis=0, keepdims=True)
            by_block = jnp.where(iota((8, 256), 0) == q, found, by_block)
        into_column = (wide_row // 8 == source_device) & (lax.rem(wide_lane, 8) == HALF + number)
        placed = placed + exact(by_block, into_column, 1, 0)
    place[...] = placed

    for n, copy in enumerate(band_loads):
        copy.wait()
        build_pairs(bands, tail, pairs, n * step_k, (n + 1) * step_k)

    def remote(src, dst, send, recv, device):
        return pltpu.make_async_remote_copy(
            src_ref=src, dst_ref=dst, send_sem=send, recv_sem=recv, device_id=device, device_id_type=MESH
        )

    def wait_bytes(ref, sem):
        pltpu.make_async_copy(ref, ref, sem).wait()

    pl.semaphore_wait(barrier, len(everyone))

    def evaluate(e, carry):
        base, now = list(carry[:8]), list(carry[8:])
        par = lax.rem(e, 2)
        comps = jnp.concatenate(now, axis=0)
        blank = jnp.zeros((64, 128), f32)
        products = dot(couple[0], jnp.concatenate([comps, blank], axis=0), 1, 1)
        products += dot(couple[1], jnp.concatenate([blank, comps], axis=0), 1, 1)

        sums = density_of(pairs, now, 0)
        tile = jnp.zeros((8, 128), f32)
        for j in range(HALF):
            tile = jnp.where(row == j, jnp.sum(sums[j], axis=0, keepdims=True), tile)
        first_recv[par, 0] = tile + products[0:8]
        for n in ORDER:
            first_send[par, n] = tile + products[8 * n : 8 * n + 8]
        for n in ORDER:
            remote(
                first_send.at[par, n], first_recv.at[par, n], send_sem.at[0, par], recv_sem.at[0, par], layer_ids[n]
            ).start()

        sums = density_of(pairs, now, 1)
        for j in range(HALF):
            second_send[par, j : j + 1] = jnp.sum(sums[j], axis=0, keepdims=True)
        for n in ORDER:
            remote(
                second_send.at[par], second_recv.at[par, n], send_sem.at[1, par], recv_sem.at[1, par], layer_ids[n]
            ).start()
        second_recv[par, 0] = second_send[par]

        def total_of(parts):
            while len(parts) > 1:
                parts = [a + b for a, b in zip(parts[0::2], parts[1::2])]
            return parts[0]

        wait_bytes(first_recv.at[par, pl.ds(1, DEVICES - 1)], recv_sem.at[0, par])
        density = total_of([first_recv[par, n] for n in range(DEVICES)])
        arrived = dot(place[...], first_recv[par].reshape(DEVICES * 8, 128), 1, 0)
        packed = gram_of(pairs, coulomb_rows[0] * density, 0)

        rows_send[par] = arrived
        for n, device in enumerate(line_ids):
            remote(
                rows_send.at[par], rows_recv.at[par, ga], send_sem.at[2, par], recv_sem.at[2 + n, par], device
            ).start()
        rows_recv[par, ga] = arrived

        wait_bytes(second_recv.at[par, pl.ds(1, DEVICES - 1)], recv_sem.at[1, par])
        density = total_of([second_recv[par, n] for n in range(DEVICES)])
        second = gram_of(pairs, coulomb_rows[1, 0:HALF] * density, 1)
        packed = [a + b for a, b in zip(packed, second)]
        for v in range(4):
            ham_send[par, v] = packed[v]
        for n, device in enumerate(line_ids):
            remote(
                ham_send.at[par], ham_recv.at[par, ga], send_sem.at[3, par], recv_sem.at[5 + n, par], device
            ).start()
        for v in range(4):
            ham_recv[par, ga, v] = packed[v]

        for n, source in enumerate(line_sources):
            wait_bytes(rows_recv.at[par, source], recv_sem.at[2 + n, par])
        all_rows = jnp.concatenate([rows_recv[par, g] for g in range(SIDE)], axis=0)
        place_row = iota((32, 128), 0)
        place_lane = lax.rem(iota((32, 128), 1), 64)
        sigma = None
        for part in range(2):
            at = lax.rem(place_row, 8) * 8 + 2 * (place_row // 8) + part
            placed = dot(all_rows, (place_lane == at).astype(f32), 0, 0)[part * 64 : part * 64 + 64]
            sigma = placed if sigma is None else sigma + placed
        field = jnp.float32(0.0)
        for s in range(2 * STEPS):
            field = jnp.where(e == s, jnp.float32(pulse_field(0.5 * time_step * s)), field)
        known = [sigma[8 * t : 8 * t + 8] + field * dipole_h[t] for t in range(8)]
        known[0] = known[0] + band_diag

        for n, source in enumerate(line_sources):
            wait_bytes(ham_recv.at[par, source], recv_sem.at[5 + n, par])
        hartree = unpacked(
            [
                (ham_recv[par, 0, v] + ham_recv[par, 1, v]) + (ham_recv[par, 2, v] + ham_recv[par, 3, v])
                for v in range(4)
            ]
        )
        ham = [h + other for h, other in zip(hartree, known)]
        change = change_of(ham, [now[0] + ground] + now[1:])
        length = jnp.where(par == 0, jnp.float32(0.5 * time_step), jnp.float32(time_step))
        new = [b + length * c for b, c in zip(base, change)]
        base = [jnp.where(par == 0, b, n) for b, n in zip(base, new)]

        wait_bytes(first_recv.at[par, pl.ds(1, DEVICES - 1)], send_sem.at[0, par])
        wait_bytes(second_recv.at[par, pl.ds(1, DEVICES - 1)], send_sem.at[1, par])
        wait_bytes(rows_recv.at[par, pl.ds(0, 3)], send_sem.at[2, par])
        wait_bytes(ham_recv.at[par, pl.ds(0, 3)], send_sem.at[3, par])
        return tuple(base) + tuple(new)

    final = lax.fori_loop(0, 2 * STEPS, evaluate, tuple(start) + tuple(start))[:8]
    out_ref[...] = dot(jnp.concatenate(final, axis=0), back_buf[...], 0, 0)[:NK]


def local(delta_rho, bloch_blocks, coulomb, energies, dipole, pair_count, pair_target, kernel_list):
    into, back = component_tables()
    hbm = pl.BlockSpec(memory_space=pltpu.HBM)
    return pl.pallas_call(
        kernel,
        out_shape=jax.ShapeDtypeStruct((NK, 128), f32),
        in_specs=[hbm] * 10,
        out_specs=pl.BlockSpec(memory_space=pltpu.VMEM),
        scratch_shapes=[
            pltpu.VMEM((NK, 128), f32),
            pltpu.VMEM((NK, 2, NB, NG), f32),
            pltpu.VMEM((NG,), f32),
            pltpu.VMEM((NB, NK), f32),
            pltpu.VMEM((NK, 128), f32),
            pltpu.VMEM((256,), jnp.int32),
            pltpu.VMEM((MAXP, 256), jnp.int32),
            pltpu.VMEM((NBLK, MAXP * KB * KB), f32),
            pltpu.VMEM((64, 128), f32),
            pltpu.VMEM((64, 128), f32),
            pltpu.VMEM((2, NK * 8, 8, HALF * 128), f32),
            pltpu.VMEM((NK, 2, 8, 128), f32),
            pltpu.VMEM((2, 256, 128), f32),
            pltpu.VMEM((2, 8, 128), f32),
            pltpu.VMEM((8, DEVICES * 8), f32),
            pltpu.VMEM((2, DEVICES, 8, 128), f32),
            pltpu.VMEM((2, DEVICES, 8, 128), f32),
            pltpu.VMEM((2, HALF, 128), f32),
            pltpu.VMEM((2, DEVICES, HALF, 128), f32),
            pltpu.VMEM((2, 8, 128), f32),
            pltpu.VMEM((2, SIDE, 8, 128), f32),
            pltpu.VMEM((2, 4, 8, 128), f32),
            pltpu.VMEM((2, SIDE, 4, 8, 128), f32),
            pltpu.SemaphoreType.DMA((9,)),
            pltpu.SemaphoreType.DMA((CHUNKS,)),
            pltpu.SemaphoreType.DMA((4, 2)),
            pltpu.SemaphoreType.DMA((8, 2)),
        ],
        compiler_params=pltpu.CompilerParams(
            collective_id=0, has_side_effects=True, vmem_limit_bytes=58 * 1024 * 1024
        ),
        name="propagate",
    )(
        delta_rho,
        bloch_blocks,
        coulomb,
        energies.T,
        dipole,
        pair_count,
        pair_target.T,
        kernel_list,
        jnp.asarray(into),
        jnp.asarray(back),
    )


def solution(mesh):
    in_specs = (
        P("ka", None),
        P("ka", None, None, "ga"),
        P("ga"),
        P("ka", None),
        P("ka", None),
        P(),
        P(),
        P(),
    )
    return jax.shard_map(local, mesh=mesh, in_specs=in_specs, out_specs=P("ka", None), check_vma=False)
```

```python
import functools
import math

import jax
import jax.numpy as jnp
import numpy as np
from jax import lax
from jax.experimental import pallas as pl
from jax.experimental.pallas import tpu as pltpu
from jax.sharding import PartitionSpec as P

NB = 8
KB = 8
MAXP = 8
STEPS = 3
NBLK = 8
NK = 64
NG = 1500
TILES = 12
SIDE = 4
CHUNKS = 8
HALF = TILES // 2
UNROLL = 64

time_step = 0.1
pulse_amp = 3.0
pulse_center = 0.15
pulse_width = 0.2
pulse_freq = 2.0
highest = lax.Precision.HIGHEST
MESH = pl.DeviceIdType.MESH
f32 = jnp.float32


def hops(step):
    return min(step, SIDE - step)


LAYER = [(a, b, c) for a in range(SIDE) for b in range(SIDE) for c in range(2)]
DEVICES = len(LAYER)
ORDER = sorted(range(1, DEVICES), key=lambda n: -(hops(LAYER[n][0]) + hops(LAYER[n][1])))
LINE = (2, 1, 3)


def pulse_field(moment):
    return (
        pulse_amp
        * math.exp(-(((moment - pulse_center) / pulse_width) ** 2))
        * math.cos(pulse_freq * moment)
    )


def component_tables():
    into = np.zeros((64, 128), np.float32)
    back = np.zeros((64, 128), np.float32)

    def real_entry(row, i, j):
        into[row, i * 8 + j] += 0.5
        into[row, j * 8 + i] += 0.5
        back[row, i * 8 + j] = 1.0
        back[row, j * 8 + i] = 1.0

    def imag_entry(row, i, j):
        into[row, 64 + i * 8 + j] += 0.5
        into[row, 64 + j * 8 + i] -= 0.5
        back[row, 64 + i * 8 + j] = 1.0
        back[row, 64 + j * 8 + i] = -1.0

    for i in range(8):
        real_entry(i, i, i)
        if i < 4:
            real_entry(8 + i, i, i + 4)
        else:
            imag_entry(8 + i, i, i - 4)
        for v in (1, 2, 3):
            real_entry(16 * v + i, i, (i + v) % 8)
            imag_entry(16 * v + 8 + i, i, (i + v) % 8)
    return into, back


def dot(a, b, lhs_dim, rhs_dim, precision=highest):
    return lax.dot_general(
        a, b, (((lhs_dim,), (rhs_dim,)), ((), ())), precision=precision, preferred_element_type=f32
    )


def iota(shape, axis):
    return lax.broadcasted_iota(jnp.int32, shape, axis)


def rolled(value, up):
    up = up % 8
    return value if up == 0 else pltpu.roll(value, 8 - up, 0)


def swap(value):
    return pltpu.roll(value, 64, 1)


def unpacked(packed):
    left = iota((8, 128), 1) < 64
    comps = []
    for value in packed:
        other = swap(value)
        comps += [jnp.where(left, value, other), jnp.where(left, other, value)]
    return comps


def offsets_of(comps):
    top = iota((8, 128), 0) < 4
    mixed = comps[1]
    turned = rolled(mixed, 4)
    real = [comps[0], comps[2], comps[4], comps[6], jnp.where(top, mixed, turned)]
    imag = [None, comps[3], comps[5], comps[7], jnp.where(top, -turned, mixed)]
    for offset in (5, 6, 7):
        real.append(rolled(real[8 - offset], offset))
        imag.append(-rolled(imag[8 - offset], offset))
    return real, imag


def change_of(hamilton, state):
    top = iota((8, 128), 0) < 4
    ham_re, ham_im = offsets_of(hamilton)
    rho_re, rho_im = offsets_of(state)

    def add(total, term):
        return term if total is None else total + term

    prod_re, prod_im = [], []
    for d in range(8):
        plus, minus, cross = None, None, None
        for e in range(8):
            f = (d - e) % 8
            re = rolled(rho_re[f], e)
            plus = add(plus, ham_re[e] * re)
            if e > 0:
                cross = add(cross, ham_im[e] * re)
            if f > 0:
                im = rolled(rho_im[f], e)
                cross = add(cross, ham_re[e] * im)
                if e > 0:
                    minus = add(minus, ham_im[e] * im)
        prod_re.append(plus - minus)
        prod_im.append(cross)
    change_re, change_im = [], []
    for d in range(5):
        other = (8 - d) % 8
        change_re.append(prod_im[d] + rolled(prod_im[other], d))
        change_im.append(rolled(prod_re[other], d) - prod_re[d])
    return [
        change_re[0],
        jnp.where(top, change_re[4], change_im[4]),
        change_re[1],
        change_im[1],
        change_re[2],
        change_im[2],
        change_re[3],
        change_im[3],
    ]


def build_pairs(bands, tail, pairs, first, last):
    top = iota((8, 128), 0) < 4

    def build(step, _):
        edge = (TILES - 1) * 128
        for k in (2 * step, 2 * step + 1):
            for part in range(2):
                tail[k, part, :, : NG - edge] = bands[k, part, :, edge:]
        for k in (2 * step, 2 * step + 1):
            for j in range(TILES):
                lanes = slice(j * 128, (j + 1) * 128)
                if j < TILES - 1:
                    u, v = bands[k, 0, :, lanes], bands[k, 1, :, lanes]
                else:
                    u, v = tail[k, 0], tail[k, 1]
                us = [u] + [rolled(u, d) for d in (1, 2, 3, 4)]
                vs = [v] + [rolled(v, d) for d in (1, 2, 3, 4)]
                values = [
                    u * u + v * v,
                    u * jnp.where(top, us[4], vs[4]) + v * jnp.where(top, vs[4], -us[4]),
                ]
                for d in (1, 2, 3):
                    values += [u * us[d] + v * vs[d], u * vs[d] - v * us[d]]
                for t, value in enumerate(values):
                    pairs[j // HALF, k * 8 + t, :, (j % HALF) * 128 : (j % HALF + 1) * 128] = value
        return 0

    lax.fori_loop(first // 2, last // 2, build, 0)


def loop(body, carry):
    return body(0, carry) if UNROLL == NK else lax.fori_loop(0, NK // UNROLL, body, carry)


def density_of(pairs, state, half):
    top = iota((8, 128), 0) < 4
    weights = [state[0], jnp.where(top, 2.0, -2.0) * state[1]]
    for v in (1, 2, 3):
        weights += [2.0 * state[2 * v], -2.0 * state[2 * v + 1]]

    def add(step, sums):
        sums = list(sums)
        for r in range(UNROLL):
            k = step * UNROLL + r
            at = jnp.full((8, 128), k, jnp.int32)
            for t in range(8):
                weight = jnp.take_along_axis(weights[t], at, axis=1, mode="promise_in_bounds")
                for j in range(HALF):
                    sums[j] = sums[j] + weight * pairs[half, k * 8 + t, :, j * 128 : (j + 1) * 128]
        return tuple(sums)

    return loop(add, (jnp.zeros((8, 128), f32),) * HALF)


def gram_of(pairs, rows, half):
    lane = iota((8, 128), 1)
    spread = [jnp.broadcast_to(rows[j : j + 1], (8, 128)) for j in range(HALF)]

    def group(step, packed):
        packed = list(packed)
        for r in range(UNROLL):
            k = step * UNROLL + r
            for t in range(8):
                total = None
                for j in range(HALF):
                    term = spread[j] * pairs[half, k * 8 + t, :, j * 128 : (j + 1) * 128]
                    total = term if total is None else total + term
                summed = jnp.broadcast_to(jnp.sum(total, axis=1, keepdims=True), (8, 128))
                packed[t // 2] = jnp.where(lane == (t % 2) * 64 + k, summed, packed[t // 2])
        return tuple(packed)

    return loop(group, (jnp.zeros((8, 128), f32),) * 4)


def kernel(
    rho_hbm, bloch_hbm, coulomb_hbm, energies_hbm, dipole_hbm, count_hbm, target_hbm, kernel_hbm, into_hbm, back_hbm,
    out_ref,
    rho_buf, bands, coulomb_buf, energies_buf, dipole_buf, count_buf, target_buf, kernel_buf, into_buf, back_buf,
    pairs, tail, couple, coulomb_rows,
    place, first_send, first_recv, second_send, second_recv, rows_send, rows_recv,
    ham_send, ham_recv,
    load_sem, band_sem, send_sem, recv_sem,
):
    ka = lax.axis_index("ka")
    ga = lax.axis_index("ga")
    core = lax.rem(ka, 2)
    chip = ka // 2
    chip_x = chip // SIDE
    chip_z = lax.rem(chip, SIDE)

    def layer_device(a, b, c):
        return (lax.rem(chip_x + a, SIDE) * SIDE + lax.rem(chip_z + b, SIDE)) * 2 + lax.rem(core + c, 2)

    layer_ids = [(layer_device(*offset), ga) for offset in LAYER]
    line_ids = [(ka, lax.rem(ga + d, SIDE)) for d in LINE]
    line_sources = [lax.rem(ga + SIDE - d, SIDE) for d in LINE]

    barrier = pltpu.get_barrier_semaphore()
    everyone = layer_ids[1:] + line_ids
    for device in everyone:
        pl.semaphore_signal(barrier, inc=1, device_id=device, device_id_type=MESH)

    step_k = NK // CHUNKS
    band_loads = [
        pltpu.make_async_copy(
            bloch_hbm.at[pl.ds(n * step_k, step_k)],
            bands.at[pl.ds(n * step_k, step_k)],
            band_sem.at[n],
        )
        for n in range(CHUNKS)
    ]
    first_block = pl.multiple_of(ka * NBLK, NBLK)
    loads = [
        pltpu.make_async_copy(src, dst, load_sem.at[n])
        for n, (src, dst) in enumerate(
            [
                (rho_hbm, rho_buf),
                (into_hbm, into_buf),
                (dipole_hbm, dipole_buf),
                (energies_hbm, energies_buf),
                (coulomb_hbm, coulomb_buf),
                (count_hbm, count_buf),
                (target_hbm, target_buf),
                (kernel_hbm.at[pl.ds(first_block, NBLK)], kernel_buf),
                (back_hbm, back_buf),
            ]
        )
    ]
    for copy in loads:
        copy.start()
    for copy in band_loads:
        copy.start()

    lane = iota((8, 128), 1)
    row = iota((8, 128), 0)
    left = lane < 64
    top = row < 4

    tail[...] = jnp.zeros((NK, 2, 8, 128), f32)
    coulomb_rows[...] = jnp.zeros((2, 8, 128), f32)

    for copy in loads:
        copy.wait()

    def components(rows):
        comps = dot(into_buf[...], jnp.concatenate([rows, rows], axis=0), 1, 1)
        return [comps[8 * t : 8 * t + 8] for t in range(8)]

    start = components(rho_buf[...])
    dipole_h = components(dipole_buf[...])
    band_diag = jnp.concatenate([energies_buf[...]] * 2, axis=1)
    ground = jnp.where(top, 1.0, 0.0)

    for j in range(TILES):
        width = min(128, NG - j * 128)
        coulomb_rows[j // HALF, j % HALF : j % HALF + 1, 0:width] = (
            coulomb_buf[j * 128 : j * 128 + width].reshape(1, width) * (1.0 / 2048.0)
        )

    def exact(a, b, lhs_dim, rhs_dim):
        return dot(a.astype(f32), b.astype(f32), lhs_dim, rhs_dim)

    target = target_buf[...]
    blocks = iota((8, 256), 1)
    counts = jnp.broadcast_to(count_buf[...].reshape(1, 256), (8, 256))
    live = iota((8, 256), 0) < counts
    wide_row = iota((256, 256), 0)
    wide_lane = iota((256, 256), 1)
    same = wide_row // 8 == wide_lane // 8
    before = same & (wide_row < wide_lane)
    lower = iota((8, 8), 1) < iota((8, 8), 0)

    own_block = (iota((256, 128), 0) == ka * 8 + lax.rem(iota((256, 128), 1), 8)) & (iota((256, 128), 1) < 64)
    on_p = row == lane // 8
    line = jnp.sum(
        jnp.where(on_p, exact(jnp.where(live, target // 8, -1), own_block, 1, 0), 0.0), axis=0, keepdims=True
    )
    square_row = iota((128, 128), 0)
    square_lane = iota((128, 128), 1)
    square = jnp.broadcast_to(line, (128, 128))
    column = jnp.sum(jnp.where(square_row == square_lane, square, 0.0), axis=1, keepdims=True)
    rank = jnp.sum(
        jnp.where((column == square) & (square_row < square_lane), 1.0, 0.0), axis=0, keepdims=True
    )
    to = iota((256, 128), 0) // 8
    to_device = (
        lax.rem(chip_x + to // 8, SIDE) * SIDE + lax.rem(chip_z + lax.rem(to // 2, SIDE), SIDE)
    ) * 2 + lax.rem(core + lax.rem(to, 2), 2)
    slot = (lax.rem(iota((256, 128), 0), 8) - HALF).astype(f32)
    hot = (line == to_device.astype(f32)) & (rank == slot) & (iota((256, 128), 1) < 64)
    entry_rows = jnp.concatenate(
        [kernel_buf[:, p * 64 : (p + 1) * 64] for p in range(MAXP)] + [jnp.zeros((64, 64), f32)], axis=0
    )
    for part in range(2):
        pick_row = iota((64, 128), 0)
        pick = (pick_row // 8 == 2 * ga + part) & (
            lax.rem(pick_row, 8) == lax.rem(iota((64, 128), 1), 8)
        )
        spread_rows = exact(entry_rows, pick, 1, 0)
        keep = (lax.rem(square_row, 8) == square_lane // 8) & (square_lane < 64)
        couple[part] = -exact(hot, jnp.where(keep, spread_rows, 0.0), 1, 0)

    mine = live & (target // 8 == ka)
    mine_f = mine.astype(f32)
    ranks = exact(mine, before, 1, 0) + exact(exact(lower, mine, 1, 0), same, 1, 0)
    source = wide_lane // 8
    source_device = (
        lax.rem(chip_x + SIDE - source // 8, SIDE) * SIDE + lax.rem(chip_z + SIDE - lax.rem(source // 2, SIDE), SIDE)
    ) * 2 + lax.rem(core + lax.rem(source, 2), 2)
    placed = jnp.zeros((8, 256), f32)
    for number in range(2):
        of_slot = jnp.where(ranks == number, mine_f, 0.0)
        by_block = jnp.zeros((8, 256), f32)
        for q in range(8):
            found = jnp.sum(jnp.where(lax.rem(target, 8) == q, of_slot, 0.0), axis=0, keepdims=True)
            by_block = jnp.where(iota((8, 256), 0) == q, found, by_block)
        into_column = (wide_row // 8 == source_device) & (lax.rem(wide_lane, 8) == HALF + number)
        placed = placed + exact(by_block, into_column, 1, 0)
    place[...] = placed

    for n, copy in enumerate(band_loads):
        copy.wait()
        build_pairs(bands, tail, pairs, n * step_k, (n + 1) * step_k)

    def remote(src, dst, send, recv, device):
        return pltpu.make_async_remote_copy(
            src_ref=src, dst_ref=dst, send_sem=send, recv_sem=recv, device_id=device, device_id_type=MESH
        )

    def wait_bytes(ref, sem):
        pltpu.make_async_copy(ref, ref, sem).wait()

    pl.semaphore_wait(barrier, len(everyone))

    def evaluate(e, carry):
        base, now = list(carry[:8]), list(carry[8:])
        par = lax.rem(e, 2)
        comps = jnp.concatenate(now, axis=0)
        blank = jnp.zeros((64, 128), f32)
        products = dot(couple[0], jnp.concatenate([comps, blank], axis=0), 1, 1)
        products += dot(couple[1], jnp.concatenate([blank, comps], axis=0), 1, 1)

        sums = density_of(pairs, now, 0)
        tile = jnp.zeros((8, 128), f32)
        for j in range(HALF):
            tile = jnp.where(row == j, jnp.sum(sums[j], axis=0, keepdims=True), tile)
        first_recv[par, 0] = tile + products[0:8]
        for n in ORDER:
            first_send[par, n] = tile + products[8 * n : 8 * n + 8]
        for n in ORDER:
            remote(
                first_send.at[par, n], first_recv.at[par, n], send_sem.at[0, par], recv_sem.at[0, par], layer_ids[n]
            ).start()

        sums = density_of(pairs, now, 1)
        for j in range(HALF):
            second_send[par, j : j + 1] = jnp.sum(sums[j], axis=0, keepdims=True)
        for n in ORDER:
            remote(
                second_send.at[par], second_recv.at[par, n], send_sem.at[1, par], recv_sem.at[1, par], layer_ids[n]
            ).start()
        second_recv[par, 0] = second_send[par]

        def total_of(parts):
            while len(parts) > 1:
                parts = [a + b for a, b in zip(parts[0::2], parts[1::2])]
            return parts[0]

        wait_bytes(first_recv.at[par, pl.ds(1, DEVICES - 1)], recv_sem.at[0, par])
        density = total_of([first_recv[par, n] for n in range(DEVICES)])
        arrived = dot(place[...], first_recv[par].reshape(DEVICES * 8, 128), 1, 0)
        packed = gram_of(pairs, coulomb_rows[0] * density, 0)

        rows_send[par] = arrived
        for n, device in enumerate(line_ids):
            remote(
                rows_send.at[par], rows_recv.at[par, ga], send_sem.at[2, par], recv_sem.at[2 + n, par], device
            ).start()
        rows_recv[par, ga] = arrived

        wait_bytes(second_recv.at[par, pl.ds(1, DEVICES - 1)], recv_sem.at[1, par])
        density = total_of([second_recv[par, n] for n in range(DEVICES)])
        second = gram_of(pairs, coulomb_rows[1, 0:HALF] * density, 1)
        packed = [a + b for a, b in zip(packed, second)]
        for v in range(4):
            ham_send[par, v] = packed[v]
        for n, device in enumerate(line_ids):
            remote(
                ham_send.at[par], ham_recv.at[par, ga], send_sem.at[3, par], recv_sem.at[5 + n, par], device
            ).start()
        for v in range(4):
            ham_recv[par, ga, v] = packed[v]

        for n, source in enumerate(line_sources):
            wait_bytes(rows_recv.at[par, source], recv_sem.at[2 + n, par])
        all_rows = jnp.concatenate([rows_recv[par, g] for g in range(SIDE)], axis=0)
        place_row = iota((32, 128), 0)
        place_lane = lax.rem(iota((32, 128), 1), 64)
        sigma = None
        for part in range(2):
            at = lax.rem(place_row, 8) * 8 + 2 * (place_row // 8) + part
            placed = dot(all_rows, (place_lane == at).astype(f32), 0, 0)[part * 64 : part * 64 + 64]
            sigma = placed if sigma is None else sigma + placed
        field = jnp.float32(0.0)
        for s in range(2 * STEPS):
            field = jnp.where(e == s, jnp.float32(pulse_field(0.5 * time_step * s)), field)
        known = [sigma[8 * t : 8 * t + 8] + field * dipole_h[t] for t in range(8)]
        known[0] = known[0] + band_diag

        for n, source in enumerate(line_sources):
            wait_bytes(ham_recv.at[par, source], recv_sem.at[5 + n, par])
        hartree = unpacked(
            [
                (ham_recv[par, 0, v] + ham_recv[par, 1, v]) + (ham_recv[par, 2, v] + ham_recv[par, 3, v])
                for v in range(4)
            ]
        )
        ham = [h + other for h, other in zip(hartree, known)]
        change = change_of(ham, [now[0] + ground] + now[1:])
        length = jnp.where(par == 0, jnp.float32(0.5 * time_step), jnp.float32(time_step))
        new = [b + length * c for b, c in zip(base, change)]
        base = [jnp.where(par == 0, b, n) for b, n in zip(base, new)]

        wait_bytes(first_recv.at[par, pl.ds(1, DEVICES - 1)], send_sem.at[0, par])
        wait_bytes(second_recv.at[par, pl.ds(1, DEVICES - 1)], send_sem.at[1, par])
        wait_bytes(rows_recv.at[par, pl.ds(0, 3)], send_sem.at[2, par])
        wait_bytes(ham_recv.at[par, pl.ds(0, 3)], send_sem.at[3, par])
        return tuple(base) + tuple(new)

    final = lax.fori_loop(0, 2 * STEPS, evaluate, tuple(start) + tuple(start))[:8]
    out_ref[...] = dot(jnp.concatenate(final, axis=0), back_buf[...], 0, 0)[:NK]


def local(delta_rho, bloch_blocks, coulomb, energies, dipole, pair_count, pair_target, kernel_list):
    into, back = component_tables()
    hbm = pl.BlockSpec(memory_space=pltpu.HBM)
    pin = functools.partial(pltpu.with_memory_space_constraint, memory_space=pltpu.HBM)
    return pl.pallas_call(
        kernel,
        out_shape=jax.ShapeDtypeStruct((NK, 128), f32),
        in_specs=[hbm] * 10,
        out_specs=pl.BlockSpec(memory_space=pltpu.VMEM),
        scratch_shapes=[
            pltpu.VMEM((NK, 128), f32),
            pltpu.VMEM((NK, 2, NB, NG), f32),
            pltpu.VMEM((NG,), f32),
            pltpu.VMEM((NB, NK), f32),
            pltpu.VMEM((NK, 128), f32),
            pltpu.VMEM((256,), jnp.int32),
            pltpu.VMEM((MAXP, 256), jnp.int32),
            pltpu.VMEM((NBLK, MAXP * KB * KB), f32),
            pltpu.VMEM((64, 128), f32),
            pltpu.VMEM((64, 128), f32),
            pltpu.VMEM((2, NK * 8, 8, HALF * 128), f32),
            pltpu.VMEM((NK, 2, 8, 128), f32),
            pltpu.VMEM((2, 256, 128), f32),
            pltpu.VMEM((2, 8, 128), f32),
            pltpu.VMEM((8, DEVICES * 8), f32),
            pltpu.VMEM((2, DEVICES, 8, 128), f32),
            pltpu.VMEM((2, DEVICES, 8, 128), f32),
            pltpu.VMEM((2, HALF, 128), f32),
            pltpu.VMEM((2, DEVICES, HALF, 128), f32),
            pltpu.VMEM((2, 8, 128), f32),
            pltpu.VMEM((2, SIDE, 8, 128), f32),
            pltpu.VMEM((2, 4, 8, 128), f32),
            pltpu.VMEM((2, SIDE, 4, 8, 128), f32),
            pltpu.SemaphoreType.DMA((9,)),
            pltpu.SemaphoreType.DMA((CHUNKS,)),
            pltpu.SemaphoreType.DMA((4, 2)),
            pltpu.SemaphoreType.DMA((8, 2)),
        ],
        compiler_params=pltpu.CompilerParams(
            collective_id=0, has_side_effects=True, vmem_limit_bytes=44 * 1024 * 1024
        ),
        name="propagate",
    )(
        *[
            pin(value)
            for value in (
                delta_rho, bloch_blocks, coulomb, energies.T, dipole, pair_count, pair_target.T, kernel_list,
                jnp.asarray(into), jnp.asarray(back),
            )
        ],
    )


def solution(mesh):
    in_specs = (
        P("ka", None),
        P("ka", None, None, "ga"),
        P("ga"),
        P("ka", None),
        P("ka", None),
        P(),
        P(),
        P(),
    )
    return jax.shard_map(local, mesh=mesh, in_specs=in_specs, out_specs=P("ka", None), check_vma=False)
```

```python
import functools
import math

import jax
import jax.numpy as jnp
import numpy as np
from jax import lax
from jax.experimental import pallas as pl
from jax.experimental.pallas import tpu as pltpu
from jax.sharding import PartitionSpec as P

NB = 8
KB = 8
MAXP = 8
STEPS = 3
NBLK = 8
NK = 64
NG = 1500
TILES = 12
SIDE = 4
CHUNKS = 8
HALF = TILES // 2
UNROLL = 64

time_step = 0.1
pulse_amp = 3.0
pulse_center = 0.15
pulse_width = 0.2
pulse_freq = 2.0
highest = lax.Precision.HIGHEST
MESH = pl.DeviceIdType.MESH
f32 = jnp.float32


def hops(step):
    return min(step, SIDE - step)


LAYER = [(a, b, c) for a in range(SIDE) for b in range(SIDE) for c in range(2)]
DEVICES = len(LAYER)
ORDER = sorted(range(1, DEVICES), key=lambda n: -(hops(LAYER[n][0]) + hops(LAYER[n][1])))
LINE = (2, 1, 3)


def pulse_field(moment):
    return (
        pulse_amp
        * math.exp(-(((moment - pulse_center) / pulse_width) ** 2))
        * math.cos(pulse_freq * moment)
    )


def component_tables():
    into = np.zeros((64, 128), np.float32)
    back = np.zeros((64, 128), np.float32)

    def real_entry(row, i, j):
        into[row, i * 8 + j] += 0.5
        into[row, j * 8 + i] += 0.5
        back[row, i * 8 + j] = 1.0
        back[row, j * 8 + i] = 1.0

    def imag_entry(row, i, j):
        into[row, 64 + i * 8 + j] += 0.5
        into[row, 64 + j * 8 + i] -= 0.5
        back[row, 64 + i * 8 + j] = 1.0
        back[row, 64 + j * 8 + i] = -1.0

    for i in range(8):
        real_entry(i, i, i)
        if i < 4:
            real_entry(8 + i, i, i + 4)
        else:
            imag_entry(8 + i, i, i - 4)
        for v in (1, 2, 3):
            real_entry(16 * v + i, i, (i + v) % 8)
            imag_entry(16 * v + 8 + i, i, (i + v) % 8)
    return into, back


def dot(a, b, lhs_dim, rhs_dim, precision=highest):
    return lax.dot_general(
        a, b, (((lhs_dim,), (rhs_dim,)), ((), ())), precision=precision, preferred_element_type=f32
    )


def iota(shape, axis):
    return lax.broadcasted_iota(jnp.int32, shape, axis)


def rolled(value, up):
    up = up % 8
    return value if up == 0 else pltpu.roll(value, 8 - up, 0)


def swap(value):
    return pltpu.roll(value, 64, 1)


def unpacked(packed):
    left = iota((8, 128), 1) < 64
    comps = []
    for value in packed:
        other = swap(value)
        comps += [jnp.where(left, value, other), jnp.where(left, other, value)]
    return comps


def offsets_of(comps):
    top = iota((8, 128), 0) < 4
    mixed = comps[1]
    turned = rolled(mixed, 4)
    real = [comps[0], comps[2], comps[4], comps[6], jnp.where(top, mixed, turned)]
    imag = [None, comps[3], comps[5], comps[7], jnp.where(top, -turned, mixed)]
    for offset in (5, 6, 7):
        real.append(rolled(real[8 - offset], offset))
        imag.append(-rolled(imag[8 - offset], offset))
    return real, imag


def change_of(hamilton, state):
    top = iota((8, 128), 0) < 4
    ham_re, ham_im = offsets_of(hamilton)
    rho_re, rho_im = offsets_of(state)

    def add(total, term):
        return term if total is None else total + term

    prod_re, prod_im = [], []
    for d in range(8):
        plus, minus, cross = None, None, None
        for e in range(8):
            f = (d - e) % 8
            re = rolled(rho_re[f], e)
            plus = add(plus, ham_re[e] * re)
            if e > 0:
                cross = add(cross, ham_im[e] * re)
            if f > 0:
                im = rolled(rho_im[f], e)
                cross = add(cross, ham_re[e] * im)
                if e > 0:
                    minus = add(minus, ham_im[e] * im)
        prod_re.append(plus - minus)
        prod_im.append(cross)
    change_re, change_im = [], []
    for d in range(5):
        other = (8 - d) % 8
        change_re.append(prod_im[d] + rolled(prod_im[other], d))
        change_im.append(rolled(prod_re[other], d) - prod_re[d])
    return [
        change_re[0],
        jnp.where(top, change_re[4], change_im[4]),
        change_re[1],
        change_im[1],
        change_re[2],
        change_im[2],
        change_re[3],
        change_im[3],
    ]


def build_pairs(bands, tail, pairs, first, last):
    top = iota((8, 128), 0) < 4

    def build(step, _):
        edge = (TILES - 1) * 128
        for k in (2 * step, 2 * step + 1):
            for part in range(2):
                tail[k, part, :, : NG - edge] = bands[k, part, :, edge:]
        for k in (2 * step, 2 * step + 1):
            for j in range(TILES):
                lanes = slice(j * 128, (j + 1) * 128)
                if j < TILES - 1:
                    u, v = bands[k, 0, :, lanes], bands[k, 1, :, lanes]
                else:
                    u, v = tail[k, 0], tail[k, 1]
                us = [u] + [rolled(u, d) for d in (1, 2, 3, 4)]
                vs = [v] + [rolled(v, d) for d in (1, 2, 3, 4)]
                values = [
                    u * u + v * v,
                    u * jnp.where(top, us[4], vs[4]) + v * jnp.where(top, vs[4], -us[4]),
                ]
                for d in (1, 2, 3):
                    values += [u * us[d] + v * vs[d], u * vs[d] - v * us[d]]
                for t, value in enumerate(values):
                    pairs[j // HALF, k * 8 + t, :, (j % HALF) * 128 : (j % HALF + 1) * 128] = value
        return 0

    lax.fori_loop(first // 2, last // 2, build, 0)


def loop(body, carry):
    return body(0, carry) if UNROLL == NK else lax.fori_loop(0, NK // UNROLL, body, carry)


def density_of(pairs, state, half):
    top = iota((8, 128), 0) < 4
    weights = [state[0], jnp.where(top, 2.0, -2.0) * state[1]]
    for v in (1, 2, 3):
        weights += [2.0 * state[2 * v], -2.0 * state[2 * v + 1]]

    def add(step, sums):
        sums = list(sums)
        for r in range(UNROLL):
            k = step * UNROLL + r
            at = jnp.full((8, 128), k, jnp.int32)
            for t in range(8):
                weight = jnp.take_along_axis(weights[t], at, axis=1, mode="promise_in_bounds")
                for j in range(HALF):
                    sums[j] = sums[j] + weight * pairs[half, k * 8 + t, :, j * 128 : (j + 1) * 128]
        return tuple(sums)

    return loop(add, (jnp.zeros((8, 128), f32),) * HALF)


def gram_of(pairs, rows, half):
    lane = iota((8, 128), 1)
    spread = [jnp.broadcast_to(rows[j : j + 1], (8, 128)) for j in range(HALF)]

    def group(step, packed):
        packed = list(packed)
        for r in range(UNROLL):
            k = step * UNROLL + r
            for t in range(8):
                total = None
                for j in range(HALF):
                    term = spread[j] * pairs[half, k * 8 + t, :, j * 128 : (j + 1) * 128]
                    total = term if total is None else total + term
                summed = jnp.broadcast_to(jnp.sum(total, axis=1, keepdims=True), (8, 128))
                packed[t // 2] = jnp.where(lane == (t % 2) * 64 + k, summed, packed[t // 2])
        return tuple(packed)

    return loop(group, (jnp.zeros((8, 128), f32),) * 4)


def kernel(
    rho_hbm, bloch_hbm, coulomb_hbm, energies_hbm, dipole_hbm, count_hbm, target_hbm, kernel_hbm, into_hbm, back_hbm,
    out_ref,
    rho_buf, bands, coulomb_buf, energies_buf, dipole_buf, count_buf, target_buf, kernel_buf, into_buf, back_buf,
    pairs, tail, couple, coulomb_rows,
    place, first_send, first_recv, second_send, second_recv, rows_send, rows_recv,
    ham_send, ham_recv,
    load_sem, band_sem, send_sem, recv_sem,
):
    ka = lax.axis_index("ka")
    ga = lax.axis_index("ga")
    core = lax.rem(ka, 2)
    chip = ka // 2
    chip_x = chip // SIDE
    chip_z = lax.rem(chip, SIDE)

    def layer_device(a, b, c):
        return (lax.rem(chip_x + a, SIDE) * SIDE + lax.rem(chip_z + b, SIDE)) * 2 + lax.rem(core + c, 2)

    layer_ids = [(layer_device(*offset), ga) for offset in LAYER]
    line_ids = [(ka, lax.rem(ga + d, SIDE)) for d in LINE]
    line_sources = [lax.rem(ga + SIDE - d, SIDE) for d in LINE]

    barrier = pltpu.get_barrier_semaphore()
    everyone = layer_ids[1:] + line_ids
    for device in everyone:
        pl.semaphore_signal(barrier, inc=1, device_id=device, device_id_type=MESH)

    step_k = NK // CHUNKS
    band_loads = [
        pltpu.make_async_copy(
            bloch_hbm.at[pl.ds(n * step_k, step_k)],
            bands.at[pl.ds(n * step_k, step_k)],
            band_sem.at[n],
        )
        for n in range(CHUNKS)
    ]
    first_block = pl.multiple_of(ka * NBLK, NBLK)
    loads = [
        pltpu.make_async_copy(src, dst, load_sem.at[n])
        for n, (src, dst) in enumerate(
            [
                (rho_hbm, rho_buf),
                (into_hbm, into_buf),
                (dipole_hbm, dipole_buf),
                (energies_hbm, energies_buf),
                (coulomb_hbm, coulomb_buf),
                (count_hbm, count_buf),
                (target_hbm, target_buf),
                (kernel_hbm.at[pl.ds(first_block, NBLK)], kernel_buf),
                (back_hbm, back_buf),
            ]
        )
    ]
    for copy in loads:
        copy.start()
    for copy in band_loads:
        copy.start()

    lane = iota((8, 128), 1)
    row = iota((8, 128), 0)
    left = lane < 64
    top = row < 4

    tail[...] = jnp.zeros((NK, 2, 8, 128), f32)
    coulomb_rows[...] = jnp.zeros((2, 8, 128), f32)

    for copy in loads:
        copy.wait()

    def components(rows):
        comps = dot(into_buf[...], jnp.concatenate([rows, rows], axis=0), 1, 1)
        return [comps[8 * t : 8 * t + 8] for t in range(8)]

    start = components(rho_buf[...])
    dipole_h = components(dipole_buf[...])
    band_diag = jnp.concatenate([energies_buf[...]] * 2, axis=1)
    ground = jnp.where(top, 1.0, 0.0)

    for j in range(TILES):
        width = min(128, NG - j * 128)
        coulomb_rows[j // HALF, j % HALF : j % HALF + 1, 0:width] = (
            coulomb_buf[j * 128 : j * 128 + width].reshape(1, width) * (1.0 / 2048.0)
        )

    def exact(a, b, lhs_dim, rhs_dim):
        return dot(a.astype(f32), b.astype(f32), lhs_dim, rhs_dim)

    target = target_buf[...]
    blocks = iota((8, 256), 1)
    counts = jnp.broadcast_to(count_buf[...].reshape(1, 256), (8, 256))
    live = iota((8, 256), 0) < counts

    own_block = (iota((256, 128), 0) == ka * 8 + lax.rem(iota((256, 128), 1), 8)) & (iota((256, 128), 1) < 64)
    on_p = row == lane // 8
    line = jnp.sum(
        jnp.where(on_p, exact(jnp.where(live, target // 8, -1), own_block, 1, 0), 0.0), axis=0, keepdims=True
    )
    square_row = iota((128, 128), 0)
    square_lane = iota((128, 128), 1)
    square = jnp.broadcast_to(line, (128, 128))
    column = jnp.sum(jnp.where(square_row == square_lane, square, 0.0), axis=1, keepdims=True)
    rank = jnp.sum(
        jnp.where((column == square) & (square_row < square_lane), 1.0, 0.0), axis=0, keepdims=True
    )
    to = iota((256, 128), 0) // 8
    to_device = (
        lax.rem(chip_x + to // 8, SIDE) * SIDE + lax.rem(chip_z + lax.rem(to // 2, SIDE), SIDE)
    ) * 2 + lax.rem(core + lax.rem(to, 2), 2)
    slot = (lax.rem(iota((256, 128), 0), 8) - HALF).astype(f32)
    hot = (line == to_device.astype(f32)) & (rank == slot) & (iota((256, 128), 1) < 64)
    entry_rows = jnp.concatenate(
        [kernel_buf[:, p * 64 : (p + 1) * 64] for p in range(MAXP)] + [jnp.zeros((64, 64), f32)], axis=0
    )
    for part in range(2):
        pick_row = iota((64, 128), 0)
        pick = (pick_row // 8 == 2 * ga + part) & (
            lax.rem(pick_row, 8) == lax.rem(iota((64, 128), 1), 8)
        )
        spread_rows = exact(entry_rows, pick, 1, 0)
        keep = (lax.rem(square_row, 8) == square_lane // 8) & (square_lane < 64)
        couple[part] = -exact(hot, jnp.where(keep, spread_rows, 0.0), 1, 0)

    for n, copy in enumerate(band_loads):
        copy.wait()
        build_pairs(bands, tail, pairs, n * step_k, (n + 1) * step_k)

    def remote(src, dst, send, recv, device):
        return pltpu.make_async_remote_copy(
            src_ref=src, dst_ref=dst, send_sem=send, recv_sem=recv, device_id=device, device_id_type=MESH
        )

    def wait_bytes(ref, sem):
        pltpu.make_async_copy(ref, ref, sem).wait()

    pl.semaphore_wait(barrier, len(everyone))

    def evaluate(e, carry):
        base, now = list(carry[:8]), list(carry[8:])
        par = lax.rem(e, 2)
        comps = jnp.concatenate(now, axis=0)
        blank = jnp.zeros((64, 128), f32)
        products = dot(couple[0], jnp.concatenate([comps, blank], axis=0), 1, 1)
        products += dot(couple[1], jnp.concatenate([blank, comps], axis=0), 1, 1)

        sums = density_of(pairs, now, 0)
        tile = jnp.zeros((8, 128), f32)
        for j in range(HALF):
            tile = jnp.where(row == j, jnp.sum(sums[j], axis=0, keepdims=True), tile)
        first_recv[par, 0] = tile + products[0:8]
        for n in ORDER:
            first_send[par, n] = tile + products[8 * n : 8 * n + 8]
        for n in ORDER:
            remote(
                first_send.at[par, n], first_recv.at[par, n], send_sem.at[0, par], recv_sem.at[0, par], layer_ids[n]
            ).start()

        sums = density_of(pairs, now, 1)
        for j in range(HALF):
            second_send[par, j : j + 1] = jnp.sum(sums[j], axis=0, keepdims=True)
        for n in ORDER:
            remote(
                second_send.at[par], second_recv.at[par, n], send_sem.at[1, par], recv_sem.at[1, par], layer_ids[n]
            ).start()
        second_recv[par, 0] = second_send[par]

        @pl.when(e == 0)
        def _():
            target = target_buf[...]
            counts = jnp.broadcast_to(count_buf[...].reshape(1, 256), (8, 256))
            wide_row = iota((256, 256), 0)
            wide_lane = iota((256, 256), 1)
            same = wide_row // 8 == wide_lane // 8
            before = same & (wide_row < wide_lane)
            lower = iota((8, 8), 1) < iota((8, 8), 0)
            mine = (iota((8, 256), 0) < counts) & (target // 8 == ka)
            mine_f = mine.astype(f32)
            ranks = exact(mine, before, 1, 0) + exact(exact(lower, mine, 1, 0), same, 1, 0)
            source = wide_lane // 8
            source_device = (
                lax.rem(chip_x + SIDE - source // 8, SIDE) * SIDE + lax.rem(chip_z + SIDE - lax.rem(source // 2, SIDE), SIDE)
            ) * 2 + lax.rem(core + lax.rem(source, 2), 2)
            placed = jnp.zeros((8, 256), f32)
            for number in range(2):
                of_slot = jnp.where(ranks == number, mine_f, 0.0)
                by_block = jnp.zeros((8, 256), f32)
                for q in range(8):
                    found = jnp.sum(jnp.where(lax.rem(target, 8) == q, of_slot, 0.0), axis=0, keepdims=True)
                    by_block = jnp.where(iota((8, 256), 0) == q, found, by_block)
                into_column = (wide_row // 8 == source_device) & (lax.rem(wide_lane, 8) == HALF + number)
                placed = placed + exact(by_block, into_column, 1, 0)
            place[...] = placed

        def total_of(parts):
            while len(parts) > 1:
                parts = [a + b for a, b in zip(parts[0::2], parts[1::2])]
            return parts[0]

        wait_bytes(first_recv.at[par, pl.ds(1, DEVICES - 1)], recv_sem.at[0, par])
        density = total_of([first_recv[par, n] for n in range(DEVICES)])
        arrived = dot(place[...], first_recv[par].reshape(DEVICES * 8, 128), 1, 0)
        packed = gram_of(pairs, coulomb_rows[0] * density, 0)

        rows_send[par] = arrived
        for n, device in enumerate(line_ids):
            remote(
                rows_send.at[par], rows_recv.at[par, ga], send_sem.at[2, par], recv_sem.at[2 + n, par], device
            ).start()
        rows_recv[par, ga] = arrived

        wait_bytes(second_recv.at[par, pl.ds(1, DEVICES - 1)], recv_sem.at[1, par])
        density = total_of([second_recv[par, n] for n in range(DEVICES)])
        second = gram_of(pairs, coulomb_rows[1, 0:HALF] * density, 1)
        packed = [a + b for a, b in zip(packed, second)]
        for v in range(4):
            ham_send[par, v] = packed[v]
        for n, device in enumerate(line_ids):
            remote(
                ham_send.at[par], ham_recv.at[par, ga], send_sem.at[3, par], recv_sem.at[5 + n, par], device
            ).start()
        for v in range(4):
            ham_recv[par, ga, v] = packed[v]

        for n, source in enumerate(line_sources):
            wait_bytes(rows_recv.at[par, source], recv_sem.at[2 + n, par])
        all_rows = jnp.concatenate([rows_recv[par, g] for g in range(SIDE)], axis=0)
        place_row = iota((32, 128), 0)
        place_lane = lax.rem(iota((32, 128), 1), 64)
        sigma = None
        for part in range(2):
            at = lax.rem(place_row, 8) * 8 + 2 * (place_row // 8) + part
            placed = dot(all_rows, (place_lane == at).astype(f32), 0, 0)[part * 64 : part * 64 + 64]
            sigma = placed if sigma is None else sigma + placed
        field = jnp.float32(0.0)
        for s in range(2 * STEPS):
            field = jnp.where(e == s, jnp.float32(pulse_field(0.5 * time_step * s)), field)
        known = [sigma[8 * t : 8 * t + 8] + field * dipole_h[t] for t in range(8)]
        known[0] = known[0] + band_diag

        for n, source in enumerate(line_sources):
            wait_bytes(ham_recv.at[par, source], recv_sem.at[5 + n, par])
        hartree = unpacked(
            [
                (ham_recv[par, 0, v] + ham_recv[par, 1, v]) + (ham_recv[par, 2, v] + ham_recv[par, 3, v])
                for v in range(4)
            ]
        )
        ham = [h + other for h, other in zip(hartree, known)]
        change = change_of(ham, [now[0] + ground] + now[1:])
        length = jnp.where(par == 0, jnp.float32(0.5 * time_step), jnp.float32(time_step))
        new = [b + length * c for b, c in zip(base, change)]
        base = [jnp.where(par == 0, b, n) for b, n in zip(base, new)]

        wait_bytes(first_recv.at[par, pl.ds(1, DEVICES - 1)], send_sem.at[0, par])
        wait_bytes(second_recv.at[par, pl.ds(1, DEVICES - 1)], send_sem.at[1, par])
        wait_bytes(rows_recv.at[par, pl.ds(0, 3)], send_sem.at[2, par])
        wait_bytes(ham_recv.at[par, pl.ds(0, 3)], send_sem.at[3, par])
        return tuple(base) + tuple(new)

    final = lax.fori_loop(0, 2 * STEPS, evaluate, tuple(start) + tuple(start))[:8]
    out_ref[...] = dot(jnp.concatenate(final, axis=0), back_buf[...], 0, 0)[:NK]


def local(delta_rho, bloch_blocks, coulomb, energies, dipole, pair_count, pair_target, kernel_list):
    into, back = component_tables()
    hbm = pl.BlockSpec(memory_space=pltpu.HBM)
    pin = functools.partial(pltpu.with_memory_space_constraint, memory_space=pltpu.HBM)
    return pl.pallas_call(
        kernel,
        out_shape=jax.ShapeDtypeStruct((NK, 128), f32),
        in_specs=[hbm] * 10,
        out_specs=pl.BlockSpec(memory_space=pltpu.VMEM),
        scratch_shapes=[
            pltpu.VMEM((NK, 128), f32),
            pltpu.VMEM((NK, 2, NB, NG), f32),
            pltpu.VMEM((NG,), f32),
            pltpu.VMEM((NB, NK), f32),
            pltpu.VMEM((NK, 128), f32),
            pltpu.VMEM((256,), jnp.int32),
            pltpu.VMEM((MAXP, 256), jnp.int32),
            pltpu.VMEM((NBLK, MAXP * KB * KB), f32),
            pltpu.VMEM((64, 128), f32),
            pltpu.VMEM((64, 128), f32),
            pltpu.VMEM((2, NK * 8, 8, HALF * 128), f32),
            pltpu.VMEM((NK, 2, 8, 128), f32),
            pltpu.VMEM((2, 256, 128), f32),
            pltpu.VMEM((2, 8, 128), f32),
            pltpu.VMEM((8, DEVICES * 8), f32),
            pltpu.VMEM((2, DEVICES, 8, 128), f32),
            pltpu.VMEM((2, DEVICES, 8, 128), f32),
            pltpu.VMEM((2, HALF, 128), f32),
            pltpu.VMEM((2, DEVICES, HALF, 128), f32),
            pltpu.VMEM((2, 8, 128), f32),
            pltpu.VMEM((2, SIDE, 8, 128), f32),
            pltpu.VMEM((2, 4, 8, 128), f32),
            pltpu.VMEM((2, SIDE, 4, 8, 128), f32),
            pltpu.SemaphoreType.DMA((9,)),
            pltpu.SemaphoreType.DMA((CHUNKS,)),
            pltpu.SemaphoreType.DMA((4, 2)),
            pltpu.SemaphoreType.DMA((8, 2)),
        ],
        compiler_params=pltpu.CompilerParams(
            collective_id=0, has_side_effects=True, vmem_limit_bytes=44 * 1024 * 1024
        ),
        name="propagate",
    )(
        *[
            pin(value)
            for value in (
                delta_rho, bloch_blocks, coulomb, energies.T, dipole, pair_count, pair_target.T, kernel_list,
                jnp.asarray(into), jnp.asarray(back),
            )
        ],
    )


def solution(mesh):
    in_specs = (
        P("ka", None),
        P("ka", None, None, "ga"),
        P("ga"),
        P("ka", None),
        P("ka", None),
        P(),
        P(),
        P(),
    )
    return jax.shard_map(local, mesh=mesh, in_specs=in_specs, out_specs=P("ka", None), check_vma=False)
```
